128 devices in a mesh: dp: 4 (over y), graph: 32 (over z, x, core).
Axes of the slice: x: 4, y: 4, z: 4, core: 2. Of those that a mesh axis runs over, the one named last changes fastest.
Arguments:
- messages: bfloat16 [4, 32768, 512], P('dp', 'graph'), may hold values from -6 to 6
- cotangent: bfloat16 [4, 32768, 512], P('dp', 'graph'), may hold values from -6 to 6
- triplet_basis: bfloat16 [4, 32768, 3584], P('dp', 'graph'), may hold values from -6 to 6
- w_edge: bfloat16 [512, 512], replicated, may hold values from -0.25 to 0.25
- w_down: bfloat16 [512, 64], replicated, may hold values from -0.25 to 0.25
- w_bil: bfloat16 [112, 4096], replicated, may hold values from -0.01171875 to 0.01171875
- w_up: bfloat16 [2, 64, 512], replicated, may hold values from -0.75 to 0.75
- trip_src: int32 [4, 32768, 32], P('dp', 'graph'), may hold values from -1 to 2047, as said below
- send_rows: int32 [4, 128, 256], P('dp', 'graph'), may hold values from 0 to 1023, as said below
- send_count: int32 [4, 128], P('dp', 'graph'), may hold values from 1 to 256, as said below
- rev_src: int32 [4, 32768], P('dp', 'graph'), may hold values from -1 to 2047, as said below
- edge_count: int32 [4, 32], P('dp', 'graph'), may hold values from 614 to 1024, as said below
Outputs:
- grad_messages: bfloat16 [4, 32768, 512], P('dp', 'graph')
- grad_w_edge: float32 [512, 512], P('graph')
- grad_w_down: float32 [512, 64], P('graph')
- grad_w_bil: float32 [112, 4096], P(None, 'graph')
- grad_w_up: float32 [2, 64, 512], P(None, None, 'graph')
The draws below stay inside these ranges and needn't reach their ends.
Inputs may be any that keep to these rules, and one draw needn't show every extreme that they name: `trip_src`: an entry below 1024 is a live edge of the same device; an entry 1024 + o * 256 + c names row c, below its count, of send list o of the device off(o) positions lower along graph (cyclically). Slots k at or beyond an edge's triplet count, and all slots of empty edges, are -1. `send_rows`: send list o of a device goes to the device off(o) positions higher along graph, cyclically. Its entries are distinct live rows; entries at or beyond the list's count are padding. `send_count`: in each slab some list holds exactly 256 rows. `rev_src`: every live edge has one reverse edge, on its own device or within 2 devices; if edge e reads row r as its reverse, the edge behind r reads e back. Empty slots hold -1. `edge_count`: in each slab some device is full.
All inputs are finite; a program needn't handle non-finite values.
Results may differ from the reference program's by a relative error of at most 0.023.
Values may be sent and summed in bfloat16 or wider, within the bound.
A program may use at most 192 MiB of HBM per device.

```python
import jax
import jax.numpy as jnp
from jax import lax

D = 512
TW = 64
NB = 112
E_DEV = 1024
K = 32
REACH = 2
CAP = 256
POOL = 2048
EDGES = 32768
SLABS = 4
N_GRAPH = 32


def offsets_drawn(count):
    return [(which // 2 + 1) * (1 - 2 * (which % 2)) for which in range(count)]


def build_slab(key):
    devices = N_GRAPH
    edges = E_DEV
    list_count = 2 * REACH
    shifts = offsets_drawn(list_count)
    keys = jax.random.split(key, 12)
    pair_half = 2 * jax.random.randint(keys[0], (devices, REACH), CAP // 8, CAP // 4 + 1)
    columns = []
    for which in range(list_count):
        reach_index = abs(shifts[which]) - 1
        if shifts[which] > 0:
            columns.append(pair_half[:, reach_index])
        else:
            columns.append(jnp.roll(pair_half[:, reach_index], -shifts[which], axis=0))
    pair_count = jnp.stack(columns, axis=1)
    block_end = jnp.cumsum(pair_count, axis=1)
    block_start = block_end - pair_count
    remote = block_end[:, -1]
    halves = jax.random.randint(keys[1], (devices,), (3 * edges + 9) // 10, edges // 2 + 1)
    chosen = jax.random.randint(keys[2], (), 0, devices)
    live_count = jnp.where(jnp.arange(devices) == chosen, edges, 2 * halves)
    canon = jnp.arange(edges)[None, :]
    block_id = jnp.sum((canon[:, :, None] >= block_end[:, None, :]).astype(jnp.int32), axis=2)
    block_clip = jnp.minimum(block_id, list_count - 1)
    within = canon - jnp.take_along_axis(block_start, block_clip, axis=1)
    is_remote = canon < remote[:, None]
    is_live = canon < live_count[:, None]
    remote_value = edges + jnp.bitwise_xor(block_clip, 1) * CAP + within
    self_partner = remote[:, None] + jnp.bitwise_xor(canon - remote[:, None], 1)
    noise = jax.random.randint(keys[3], (devices, edges), 0, 2 ** 16) * edges + canon
    order_key = jnp.where(is_live, noise, 2 ** 16 * edges + canon)
    order = jnp.argsort(order_key, axis=1)
    new_place = jnp.argsort(order, axis=1).astype(jnp.int32)
    self_new = jnp.take_along_axis(new_place, jnp.clip(self_partner, 0, edges - 1), axis=1)
    rev_canon = jnp.where(is_remote, remote_value, jnp.where(is_live, self_new, -1))
    rev_new = jnp.zeros((devices, edges), jnp.int32)
    rev_new = jax.vmap(lambda target, placed, values: target.at[placed].set(values))(rev_new, new_place, rev_canon.astype(jnp.int32))
    pick_noise = jax.random.randint(keys[4], (devices, list_count, edges), 0, 2 ** 16) * edges + canon[:, None, :]
    in_block = (block_id[:, None, :] == jnp.arange(list_count)[None, :, None]) & is_remote[:, None, :]
    pick_key = jnp.where(in_block, within[:, None, :], jnp.where(is_live[:, None, :], edges + pick_noise, 2 ** 17 * edges + canon[:, None, :]))
    picked = jnp.argsort(pick_key, axis=2)[:, :, :CAP]
    send_lists = jax.vmap(lambda placed, chosen_rows: placed[chosen_rows])(new_place, picked)
    extra = jax.random.randint(keys[5], (devices, list_count), 1, CAP - pair_count + 1)
    counts = pair_count + extra
    full_device = jax.random.randint(keys[6], (), 0, devices)
    full_list = jax.random.randint(keys[7], (), 0, list_count)
    counts = jnp.where((jnp.arange(devices)[:, None] == full_device) & (jnp.arange(list_count)[None, :] == full_list), CAP, counts)
    arrive_count = jnp.stack([jnp.roll(counts[:, which], shifts[which], axis=0) for which in range(list_count)], axis=1)
    per_edge = jax.random.randint(keys[8], (devices, edges), K // 4, K + 1)
    lane = jax.random.randint(keys[9], (devices, edges, K), 0, 2 * list_count)
    local_pick = jax.random.randint(keys[10], (devices, edges, K), 0, live_count[:, None, None])
    block_pick = jnp.clip(lane - list_count, 0, list_count - 1)
    limit = jnp.take_along_axis(arrive_count, block_pick.reshape(devices, -1), axis=1).reshape(devices, edges, K)
    slot_pick = jax.random.randint(keys[11], (devices, edges, K), 0, limit)
    source = jnp.where(lane < list_count, local_pick, edges + block_pick * CAP + slot_pick)
    used = (jnp.arange(K)[None, None, :] < per_edge[:, :, None]) & (jnp.arange(edges)[None, :, None] < live_count[:, None, None])
    trips = jnp.where(used, source, -1)
    return (trips.reshape(devices * edges, K), send_lists.reshape(devices * list_count, CAP), counts.reshape(devices * list_count), rev_new.reshape(devices * edges), live_count)


def build_all(key):
    slab_keys = jax.random.split(jax.random.fold_in(key, 31), SLABS)
    return jax.vmap(build_slab)(slab_keys)


def draw_trip_src(key, part):
    return build_all(key)[0].astype(jnp.int32)


def draw_send_rows(key, part):
    return build_all(key)[1].astype(jnp.int32)


def draw_send_count(key, part):
    return build_all(key)[2].astype(jnp.int32)


def draw_rev_src(key, part):
    return build_all(key)[3].astype(jnp.int32)


def draw_edge_count(key, part):
    return build_all(key)[4].astype(jnp.int32)


def block_scale(rng, dims, shards, low, top_value):
    factor_of = 1.0
    for position, blocks in shards:
        steps = jax.random.uniform(jax.random.fold_in(jax.random.fold_in(rng, 6), position), (blocks,), jnp.float32, low / len(shards), top_value / len(shards))
        factor_of = factor_of * jnp.repeat(jnp.exp(steps), dims[position] // blocks).reshape((-1,) + (1,) * (len(dims) - 1 - position))
    return factor_of


def scatter_about(key, dims, deviation, reach, shards=(), kind=jnp.bfloat16):
    drawn = jax.random.normal(key, dims, jnp.float32) * deviation
    if len(shards) > 0:
        drawn = block_scale(key, dims, shards, -0.22, 0.18) * drawn
    return jnp.clip(drawn, min=-reach, max=reach).astype(kind)


def setup_inputs(seed: int = 0) -> dict:
    key_of = jax.random.split(jax.random.key(seed), 13)
    return {
        "messages": scatter_about(key_of[0], (SLABS, EDGES, D), 1.0, 6.0, ((0, 4), (1, 32))),
        "cotangent": scatter_about(key_of[1], (SLABS, EDGES, D), 1.0, 6.0, ((0, 4), (1, 32))),
        "triplet_basis": scatter_about(key_of[2], (SLABS, EDGES, K * NB), 1.0, 6.0, ((0, 4), (1, 32))),
        "w_edge": scatter_about(key_of[3], (D, D), D ** -0.5, 0.25),
        "w_down": scatter_about(key_of[4], (D, TW), D ** -0.5, 0.25),
        "w_bil": scatter_about(key_of[5], (NB, TW * TW), (NB * TW * K) ** -0.5, 0.01171875),
        "w_up": scatter_about(key_of[6], (2, TW, D), TW ** -0.5, 0.75),
        "trip_src": draw_trip_src(jax.random.fold_in(key_of[12], 71), 0),
        "send_rows": draw_send_rows(jax.random.fold_in(key_of[12], 71), 0),
        "send_count": draw_send_count(jax.random.fold_in(key_of[12], 71), 0),
        "rev_src": draw_rev_src(jax.random.fold_in(key_of[12], 71), 0),
        "edge_count": draw_edge_count(jax.random.fold_in(key_of[12], 71), 0),
    }


inv_root = 0.7071067811865476

def silu_slope(values):
    sigma = jax.nn.sigmoid(values)
    return sigma * (1.0 + values * (1.0 - sigma))

def offsets(count):
    return [(which // 2 + 1) * (1 - 2 * (which % 2)) for which in range(count)]

def contract(left, right):
    return lax.dot_general(left, right, (((0,), (0,)), ((), ())), preferred_element_type=jnp.float32)

def slab_terms(messages, cotangent, triplet_basis, w_edge, w_down, w_bil, w_up, trip_src, send_rows, send_count, rev_src, edge_count):
    list_count = 2 * REACH
    shifts = offsets(list_count)
    alive = jnp.arange(E_DEV)[None, :] < edge_count[:, None]
    pre_edge = jnp.dot(messages, w_edge, preferred_element_type=jnp.float32)
    hidden = jax.nn.silu(pre_edge).astype(jnp.bfloat16)
    pre_down = jnp.dot(hidden, w_down, preferred_element_type=jnp.float32)
    reduced = jax.nn.silu(pre_down).astype(jnp.bfloat16)
    list_rows = send_rows.reshape(N_GRAPH, list_count * CAP)
    filled = jnp.arange(CAP)[None, None, :] < send_count.reshape(N_GRAPH, list_count)[:, :, None]

    def pooled(values):
        columns = values.shape[-1]
        local = values.reshape(N_GRAPH, E_DEV, columns)
        sent = jax.vmap(lambda table, picks: table[picks])(local, list_rows)
        sent = sent.reshape(N_GRAPH, list_count, CAP, columns)
        sent = jnp.where(filled[:, :, :, None], sent, jnp.zeros((), values.dtype))
        blocks = [jnp.roll(sent[:, which], shifts[which], axis=0) for which in range(list_count)]
        return jnp.concatenate([local] + blocks, axis=1)
    pool_red = pooled(reduced)
    pool_cot = pooled(cotangent)
    trips = trip_src.reshape(N_GRAPH, E_DEV, K)
    revs = rev_src.reshape(N_GRAPH, E_DEV)
    bases = triplet_basis.reshape(N_GRAPH, E_DEV, K, NB)
    cots = cotangent.reshape(N_GRAPH, E_DEV, D)
    w_flat = w_bil.reshape(NB * TW, TW)

    def device_step(totals, item):
        pool_rows, pool_cots, basis, trip, reverse, own_cot, live_rows = item
        valid = trip >= 0
        gathered = jnp.where(valid[:, :, None], pool_rows[jnp.maximum(trip, 0)], jnp.zeros((), jnp.bfloat16))
        outer = jnp.einsum('ekb,ekc->ebc', basis.astype(jnp.float32), gathered.astype(jnp.float32))
        outer = outer.astype(jnp.bfloat16).reshape(E_DEV, NB * TW)
        state = jnp.dot(outer, w_flat, preferred_element_type=jnp.float32).astype(jnp.bfloat16)
        scaled = jnp.where(live_rows[:, None], own_cot.astype(jnp.float32) * inv_root, 0.0)
        pre_ca = jnp.dot(state, w_up[0], preferred_element_type=jnp.float32)
        grad_ca = (scaled * silu_slope(pre_ca)).astype(jnp.bfloat16)
        has_rev = reverse >= 0
        mirror = jnp.where(has_rev[:, None], pool_cots[jnp.maximum(reverse, 0)], jnp.zeros((), jnp.bfloat16))
        pre_ac = jnp.dot(state, w_up[1], preferred_element_type=jnp.float32)
        grad_ac = (mirror.astype(jnp.float32) * inv_root * silu_slope(pre_ac)).astype(jnp.bfloat16)
        up_ca = contract(state, grad_ca)
        up_ac = contract(state, grad_ac)
        back_rev = jnp.dot(grad_ac, w_up[1].T, preferred_element_type=jnp.float32).astype(jnp.bfloat16)
        back_rev = lax.optimization_barrier(back_rev).astype(jnp.float32)
        grad_state = (jnp.dot(grad_ca, w_up[0].T, preferred_element_type=jnp.float32) + back_rev).astype(jnp.bfloat16)
        grad_outer = jnp.dot(grad_state, w_flat.T, preferred_element_type=jnp.float32).astype(jnp.bfloat16)
        bil = contract(outer, grad_state)
        grad_trip = jnp.einsum('ebc,ekb->ekc', grad_outer.reshape(E_DEV, NB, TW).astype(jnp.float32), basis.astype(jnp.float32))
        grad_trip = jnp.where(valid[:, :, None], grad_trip, 0.0)
        grad_pool = jnp.zeros((POOL, TW), jnp.float32).at[jnp.maximum(trip, 0).reshape(-1)].add(grad_trip.reshape(-1, TW))
        return ((totals[0] + up_ca, totals[1] + up_ac, totals[2] + bil), grad_pool)
    start = (jnp.zeros((TW, D), jnp.float32), jnp.zeros((TW, D), jnp.float32), jnp.zeros((NB * TW, TW), jnp.float32))
    totals, grad_pool = lax.scan(device_step, start, (pool_red, pool_cot, bases, trips, revs, cots, alive))
    returned = grad_pool[:, E_DEV:].reshape(N_GRAPH, list_count, CAP, TW).astype(jnp.bfloat16)
    returned = lax.optimization_barrier(returned)
    grad_red = grad_pool[:, :E_DEV]
    rows_split = list_rows.reshape(N_GRAPH, list_count, CAP)
    for which in range(list_count):
        back = jnp.roll(returned[:, which], -shifts[which], axis=0).astype(jnp.float32)
        back = jnp.where(filled[:, which, :, None], back, 0.0)
        grad_red = jax.vmap(lambda target, picks, addend: target.at[picks].add(addend))(grad_red, rows_split[:, which], back)
    grad_red = grad_red.reshape(EDGES, TW)
    grad_down = (grad_red * silu_slope(pre_down)).astype(jnp.bfloat16)
    down_sum = contract(hidden, grad_down)
    grad_hidden = jnp.dot(grad_down, w_down.T, preferred_element_type=jnp.float32)
    grad_edge = (grad_hidden * silu_slope(pre_edge)).astype(jnp.bfloat16)
    edge_sum = contract(messages, grad_edge)
    grad_messages = jnp.dot(grad_edge, w_edge.T, preferred_element_type=jnp.float32).astype(jnp.bfloat16)
    return (grad_messages, edge_sum, down_sum, totals[2], jnp.stack([totals[0], totals[1]]))

def reference(messages, cotangent, triplet_basis, w_edge, w_down, w_bil, w_up, trip_src, send_rows, send_count, rev_src, edge_count):
    outputs = []
    edge_total = jnp.zeros((D, D), jnp.float32)
    down_total = jnp.zeros((D, TW), jnp.float32)
    bil_total = jnp.zeros((NB * TW, TW), jnp.float32)
    up_total = jnp.zeros((2, TW, D), jnp.float32)
    for slab in range(SLABS):
        grad_messages, edge_sum, down_sum, bil, up_sum = slab_terms(messages[slab], cotangent[slab], triplet_basis[slab], w_edge, w_down, w_bil, w_up, trip_src[slab], send_rows[slab], send_count[slab], rev_src[slab], edge_count[slab])
        outputs.append(grad_messages)
        edge_total = edge_total + edge_sum
        down_total = down_total + down_sum
        bil_total = bil_total + bil
        up_total = up_total + up_sum
    factor = 1.0 / jnp.sqrt(jnp.float32(SLABS * EDGES))
    return (jnp.stack(outputs), edge_total * factor, down_total * factor, bil_total.reshape(NB, TW * TW) * factor, up_total * factor)
```

```python
import functools
import math

import jax
import jax.numpy as jnp
from jax import lax
from jax.experimental import pallas as pl
from jax.experimental.pallas import tpu as pltpu
from jax.sharding import PartitionSpec as P

INV_ROOT = 0.7071067811865476
BF = jnp.bfloat16
F32 = jnp.float32
MESH = pl.DeviceIdType.MESH
VMEM_LIMIT = 56 * 1024 * 1024

E = 1024
K = 32
B = 112
TW = 64
D = 512
CAP = 256
NL = 4
G = 8
T = G * K


def offsets(count):
    return [(which // 2 + 1) * (1 - 2 * (which % 2)) for which in range(count)]


def shifted(block, axis, distance):
    n = lax.axis_size(axis)
    return lax.ppermute(block, axis, [((i - distance) % n, i) for i in range(n)])


def sigmoid(v):
    return 1.0 / (1.0 + jnp.exp(-v))


def silu(v):
    return v * sigmoid(v)


def slope(v):
    s = sigmoid(v)
    return s * (1.0 + v * (1.0 - s))


def iota(shape, dim):
    return lax.broadcasted_iota(jnp.int32, shape, dim)


def dot(a, b):
    return jnp.dot(a, b, preferred_element_type=F32)


def dot_nt(a, b):
    return lax.dot_general(a, b, (((1,), (1,)), ((), ())), preferred_element_type=F32)


def dot_tn(a, b):
    return lax.dot_general(a, b, (((0,), (0,)), ((), ())), preferred_element_type=F32)


def onehot(cond):
    return jnp.where(cond, 1.0, 0.0).astype(BF)


def front_kernel(msg, cot, w_edge, w_down, rows, count, *outs):
    pool_out = outs[0]
    red_out = outs[1:5]
    cot_out = outs[5:9]
    red = outs[9]

    for i in range(4):
        m = pl.ds(256 * i, 256)
        hidden = silu(dot(msg[m, :], w_edge[...])).astype(BF)
        red[m, :] = silu(dot(hidden, w_down[...])).astype(BF)
        r = red[m, :]
        pool_out[i] = jnp.concatenate([r[:128], r[128:]], axis=1)
    lane = iota((1, CAP), 1)
    lists = []
    for o in range(NL):
        lists.append(jnp.where(lane < count[0, o], rows[o : o + 1, :], -1))
    picks = jnp.concatenate(lists + lists, axis=0).T
    wide = iota((CAP, E), 1)
    for o in range(NL):
        hot = onehot(wide == picks[:, o : o + 1])
        r = dot(hot, red[...]).astype(BF)
        red_out[o][...] = jnp.concatenate([r[:128], r[128:]], axis=1)
        cot_out[o][...] = dot(hot, cot[...]).astype(BF)


def front(msg, cot, w_edge, w_down, rows, count):
    vm = pl.BlockSpec(memory_space=pltpu.VMEM)
    return pl.pallas_call(
        front_kernel,
        out_shape=[jax.ShapeDtypeStruct((4, 128, 128), BF)]
        + [jax.ShapeDtypeStruct((128, 128), BF)] * 4
        + [jax.ShapeDtypeStruct((CAP, D), BF)] * 4,
        in_specs=[vm] * 5 + [pl.BlockSpec(memory_space=pltpu.SMEM)],
        out_specs=[vm] * 9,
        scratch_shapes=[pltpu.VMEM((E, TW), BF)],
        compiler_params=pltpu.CompilerParams(vmem_limit_bytes=VMEM_LIMIT),
        name="front",
    )(msg, cot, w_edge, w_down, rows, count)


GS = 8
GP = 4
STEPS = E // (G * GS)


def load_w(wp, w_bil):
    wp[...] = jnp.zeros_like(wp)
    for ch in range(16):
        wp[128 * ch : 128 * ch + B, :] = w_bil[:, 256 * ch : 256 * ch + 256]


def fwd_kernel(basis, idx, pool, r0, r1, r2, r3, w_bil, outer, bas, state, pool_t, wp, sbuf):
    @pl.when(pl.program_id(0) == 0)
    def _():
        load_w(wp, w_bil)
        for hi in range(8):
            src = pool[hi] if hi < 4 else (r0, r1, r2, r3)[hi - 4][...]
            flip = src.astype(F32).T
            pool_t[64 * hi : 64 * hi + 64, :] = jnp.concatenate(
                [flip[:64], flip[64:]], axis=1
            ).astype(BF)

    e_lane = lax.rem(iota((16, T), 1), G)
    quad = iota((16, T), 0) // 4
    keep = [onehot(e_lane == 4 * q + quad) for q in range(2)]
    low = iota((8, T), 0) < 4

    def some(j, carry):
        hots, his = [], []
        for i in range(GP):
            row = idx[pl.ds(j * GP + i, 1), :]
            hots.append(onehot(iota((256, T), 0) == jnp.bitwise_and(row, 255)))
            his.append(jnp.right_shift(row, 8))
        found = dot(pool_t[...], jnp.concatenate(hots, axis=1))
        for i in range(GP):
            g = j * GP + i
            wide = basis[pl.ds(pl.multiple_of(g * G, G), G), :].astype(F32)
            pieces = []
            for k in range(K):
                piece = wide[:, k * B : (k + 1) * B]
                pieces.append(jnp.concatenate([piece, jnp.zeros((G, 128 - B), F32)], axis=1))
            rhs = jnp.concatenate(pieces, axis=0).astype(BF)
            bas[pl.ds(pl.multiple_of(g * T, T), T), :] = rhs
            got = jnp.zeros((TW, T), F32)
            for hi in range(8):
                part = found[64 * hi : 64 * hi + 64, T * i : T * i + T]
                got = jnp.where(his[i] == hi, part, got)
            tiles = []
            for v in range(8):
                x = got[8 * v : 8 * v + 8]
                y = pltpu.roll(x, 4, 0)
                for d in (jnp.where(low, x, y), jnp.where(low, y, x)):
                    tiles.append(jnp.concatenate([d, d], axis=0).astype(BF))
            lhs = jnp.concatenate([t * keep[q] for q in range(2) for t in tiles], axis=0)
            out = dot(lhs, rhs).astype(BF)
            for q in range(2):
                for ch in range(16):
                    at = (q * 16 + ch) * 16
                    outer[pl.ds(pl.multiple_of(g * 32 + 16 * q, 16), 16), 128 * ch : 128 * ch + 128] = (
                        out[at : at + 16]
                    )
        return carry

    lax.fori_loop(0, GS // GP, some, 0)
    rows = 32 * GS
    full = dot(outer[...], wp[...])
    full = jnp.where(lax.rem(iota((rows, 256), 0), 4) == iota((rows, 256), 1) // 64, full, 0.0)
    full = full + pltpu.roll(full, 1, 0)
    full = full + pltpu.roll(full, 2, 0)
    sbuf[...] = full[:, :128] + full[:, 128:]
    picked = sbuf[pl.ds(3, G * GS, stride=4), :]
    state[...] = (picked + pltpu.roll(picked, 64, 1)).astype(BF)


def fwd(basis, idx, pool, recv, w_bil):
    whole = lambda shape: pl.BlockSpec(shape, lambda i: (0,) * len(shape))
    return pl.pallas_call(
        fwd_kernel,
        grid=(STEPS,),
        out_shape=[
            jax.ShapeDtypeStruct((4 * E, 2048), BF),
            jax.ShapeDtypeStruct((E * K, 128), BF),
            jax.ShapeDtypeStruct((E, 128), BF),
        ],
        in_specs=[
            pl.BlockSpec((G * GS, K * B), lambda i: (i, 0)),
            pl.BlockSpec((GS, T), lambda i: (i, 0)),
            whole((4, 128, 128)),
        ]
        + [whole((128, 128))] * 4
        + [whole((B, 4096))],
        out_specs=[
            pl.BlockSpec((32 * GS, 2048), lambda i: (i, 0)),
            pl.BlockSpec((T * GS, 128), lambda i: (i, 0)),
            pl.BlockSpec((G * GS, 128), lambda i: (i, 0)),
        ],
        scratch_shapes=[
            pltpu.VMEM((512, 256), BF),
            pltpu.VMEM((2048, 256), BF),
            pltpu.VMEM((32 * GS, 128), F32),
        ],
        compiler_params=pltpu.CompilerParams(vmem_limit_bytes=VMEM_LIMIT),
        cost_estimate=pl.CostEstimate(flops=2 * 10**10, bytes_accessed=3 * 10**7, transcendentals=0),
        name="triplets_out",
    )(basis, idx, pool, *recv, w_bil)


BE = 128


def mid_kernel(factor, state, outer, cot, all_cot, c0, c1, c2, c3, rev, w_up, count, gsx, early, bil, up):
    step = pl.program_id(0)

    @pl.when(step == 0)
    def _():
        bil[...] = jnp.zeros_like(bil)
        up[...] = jnp.zeros_like(up)

    st = state[...][:, :TW]
    alive = iota((BE, D), 0) + step * BE < count[0, 0]
    scaled = jnp.where(alive, cot[...].astype(F32) * INV_ROOT, 0.0)
    grad_ca = (scaled * slope(dot(st, w_up[0]))).astype(BF)
    row = rev[pl.ds(step, 1), :]
    col = jnp.concatenate([row] * 8, axis=0).T[:, :1]
    mirror = dot(onehot(iota((BE, E), 1) == col), all_cot[...])
    for o, c in enumerate((c0, c1, c2, c3)):
        mirror = mirror + dot(onehot(iota((BE, CAP), 1) + (E + CAP * o) == col), c[...])
    grad_ac = (mirror * INV_ROOT * slope(dot(st, w_up[1]))).astype(BF)
    up[:TW, :] += dot_tn(st, grad_ca)
    up[TW:, :] += dot_tn(st, grad_ac)
    own = dot_nt(grad_ca, jnp.concatenate([w_up[0]] * 4, axis=0))
    back = dot_nt(grad_ac, jnp.concatenate([w_up[1]] * 4, axis=0)).astype(BF)
    grad_state = (own + back.astype(F32)).astype(BF)
    spread = onehot(iota((4 * BE, BE), 0) // 4 == iota((4 * BE, BE), 1))
    big = dot(spread, grad_state)
    big = jnp.where(lax.rem(iota((4 * BE, 256), 0), 4) == iota((4 * BE, 256), 1) // 64, big, 0.0)
    big = big.astype(BF)
    gsx[...] = big
    bil[...] += dot_tn(big, outer[...])

    @pl.when(step == pl.num_programs(0) - 1)
    def _():
        turned = (up[...] * factor).T.astype(BF)
        for i in range(32):
            early[i, :, 1024:1152] = turned[16 * i : 16 * i + 16]
            r, c = (i % 2) * 128, (i // 2) * 128
            for j in range(8):
                early[i, :, 128 * j : 128 * j + 128] = (
                    bil[r + 16 * j : r + 16 * j + 16, c : c + 128] * factor
                ).astype(BF)


def mid(factor, state, outer, cot, recv, rev, w_up, count):
    whole = lambda shape: pl.BlockSpec(shape, lambda i: (0,) * len(shape))
    return pl.pallas_call(
        functools.partial(mid_kernel, factor),
        grid=(E // BE,),
        out_shape=[
            jax.ShapeDtypeStruct((4 * E, 256), BF),
            jax.ShapeDtypeStruct((32, 16, 1152), BF),
        ],
        in_specs=[
            pl.BlockSpec((BE, 128), lambda i: (i, 0)),
            pl.BlockSpec((4 * BE, 2048), lambda i: (i, 0)),
            pl.BlockSpec((BE, D), lambda i: (i, 0)),
            whole((E, D)),
        ]
        + [whole((CAP, D))] * 4
        + [whole((8, 128)), whole((2, TW, D)), pl.BlockSpec(memory_space=pltpu.SMEM)],
        out_specs=[
            pl.BlockSpec((4 * BE, 256), lambda i: (i, 0)),
            whole((32, 16, 1152)),
        ],
        scratch_shapes=[pltpu.VMEM((256, 2048), F32), pltpu.VMEM((2 * TW, D), F32)],
        compiler_params=pltpu.CompilerParams(vmem_limit_bytes=VMEM_LIMIT),
        name="middle",
    )(state, outer, cot, cot, *recv, rev, w_up, count)


def bwd_kernel(gsx, bas, idx, w_bil, local, b0, b1, b2, b3, wp, go, acc):
    step = pl.program_id(0)

    @pl.when(step == 0)
    def _():
        load_w(wp, w_bil)
        acc[...] = jnp.zeros_like(acc)

    go[...] = dot_nt(gsx[...], wp[...]).astype(BF)
    e_lane = lax.rem(iota((8, T), 1), G)
    pair = e_lane // 2
    odd = lax.rem(e_lane, 2) == 1
    stay = (iota((8, T), 0) >= 4) == odd

    def some(j, carry):
        hots, sides = [], []
        for i in range(GP):
            g = j * GP + i
            row = idx[pl.ds(g, 1), :]
            hots.append(onehot(iota((256, T), 0) == jnp.bitwise_and(row, 255)))
            hi_of = jnp.right_shift(row, 8)
            lhs = jnp.concatenate(
                [
                    go[pl.ds(pl.multiple_of(g * 32 + 16 * q, 16), 16), 128 * ch : 128 * ch + 128]
                    for q in range(2)
                    for ch in range(16)
                ],
                axis=0,
            )
            full = dot_nt(lhs, bas[pl.ds(pl.multiple_of(g * T, T), T), :])
            picked = []
            for ch in range(16):
                z = full[16 * ch : 16 * ch + 8]
                for p in range(1, 4):
                    at = (p // 2) * 256 + 16 * ch + 8 * (p % 2)
                    z = jnp.where(pair == p, full[at : at + 8], z)
                picked.append(z)
            grads = []
            for v in range(8):
                z0, z1 = picked[2 * v], picked[2 * v + 1]
                here = jnp.where(odd, z1, z0)
                there = jnp.where(odd, z0, z1)
                grads.append(jnp.where(stay, here, pltpu.roll(there, 4, 0)))
            grad = jnp.concatenate(grads, axis=0).astype(BF)
            sides.append(
                jnp.concatenate([grad * onehot(hi_of == hi) for hi in range(8)], axis=0)
            )
        acc[...] += dot_nt(jnp.concatenate(sides, axis=1), jnp.concatenate(hots, axis=1))
        return carry

    lax.fori_loop(0, GS // GP, some, 0)

    @pl.when(step == pl.num_programs(0) - 1)
    def _():
        for hi in range(8):
            part = acc[64 * hi : 64 * hi + 64, :]
            flip = jnp.concatenate([part[:, :128], part[:, 128:]], axis=0).T
            if hi < 4:
                local[hi] = flip
            else:
                (b0, b1, b2, b3)[hi - 4][...] = flip.astype(BF)


def bwd(gsx, bas, idx, w_bil):
    whole = lambda shape: pl.BlockSpec(shape, lambda i: (0,) * len(shape))
    return pl.pallas_call(
        bwd_kernel,
        grid=(STEPS,),
        out_shape=[jax.ShapeDtypeStruct((4, 128, 128), F32)]
        + [jax.ShapeDtypeStruct((128, 128), BF)] * 4,
        in_specs=[
            pl.BlockSpec((32 * GS, 256), lambda i: (i, 0)),
            pl.BlockSpec((T * GS, 128), lambda i: (i, 0)),
            pl.BlockSpec((GS, T), lambda i: (i, 0)),
            whole((B, 4096)),
        ],
        out_specs=[whole((4, 128, 128))] + [whole((128, 128))] * 4,
        scratch_shapes=[
            pltpu.VMEM((2048, 256), BF),
            pltpu.VMEM((32 * GS, 2048), BF),
            pltpu.VMEM((512, 256), F32),
        ],
        compiler_params=pltpu.CompilerParams(vmem_limit_bytes=VMEM_LIMIT),
        name="triplets_back",
    )(gsx, bas, idx, w_bil)


def tail_kernel(factor, msg, w_edge, w_down, rows, count, local, b0, b1, b2, b3, grad_msg, late, gred, edge, down):
    lane = iota((1, CAP), 1)
    hots, backs = [], []
    for o, b in enumerate((b0, b1, b2, b3)):
        picks = jnp.where(lane < count[0, o], rows[o : o + 1, :], -1)
        hots.append(onehot(iota((E, CAP), 0) == picks))
        back = b[...]
        backs.append(jnp.concatenate([back[:, :TW], back[:, TW:]], axis=0))
    gred[...] = dot(jnp.concatenate(hots, axis=1), jnp.concatenate(backs, axis=0))
    for i in range(4):
        m = pl.ds(256 * i, 256)
        own = local[i]
        total = gred[m, :] + jnp.concatenate([own[:, :TW], own[:, TW:]], axis=0)
        pre_edge = dot(msg[m, :], w_edge[...])
        hidden = silu(pre_edge).astype(BF)
        pre_down = dot(hidden, w_down[...])
        grad_down = (total * slope(pre_down)).astype(BF)
        grad_hidden = dot_nt(grad_down, w_down[...])
        grad_edge = (grad_hidden * slope(pre_edge)).astype(BF)
        grad_msg[m, :] = dot_nt(grad_edge, w_edge[...]).astype(BF)
        d = dot_tn(hidden, grad_down)
        e = dot_tn(msg[m, :], grad_edge)
        if i == 0:
            edge[...] = e
            down[...] = d
        else:
            edge[...] += e
            down[...] += d
    both = jnp.concatenate(
        [edge[...] * factor, down[...] * factor, jnp.zeros((D, TW), F32)], axis=1
    ).astype(BF)
    for i in range(32):
        late[i] = both[16 * i : 16 * i + 16]


def tail(factor, msg, w_edge, w_down, rows, count, local, back):
    vm = pl.BlockSpec(memory_space=pltpu.VMEM)
    return pl.pallas_call(
        functools.partial(tail_kernel, factor),
        out_shape=[
            jax.ShapeDtypeStruct((E, D), BF),
            jax.ShapeDtypeStruct((32, 16, 640), BF),
        ],
        in_specs=[vm] * 4 + [pl.BlockSpec(memory_space=pltpu.SMEM)] + [vm] * 5,
        out_specs=[vm] * 2,
        scratch_shapes=[
            pltpu.VMEM((E, TW), F32),
            pltpu.VMEM((D, D), F32),
            pltpu.VMEM((D, TW), F32),
        ],
        compiler_params=pltpu.CompilerParams(vmem_limit_bytes=VMEM_LIMIT),
        name="tail",
    )(msg, w_edge, w_down, rows, count, local, *back)


def sum_kernel(n, n_dp, early, late, o_edge, o_down, o_bil, o_up,
               in_e, in_l, mine_e, mine_l, dp_e, dp_l, send, recv, dp_send, dp_recv):
    me = lax.axis_index("graph")
    dp = lax.axis_index("dp")

    barrier = pltpu.get_barrier_semaphore()

    def greet(d, carry):
        pl.semaphore_signal(
            barrier, inc=1, device_id=(dp, lax.rem(me + d, n)), device_id_type=MESH
        )
        return carry

    lax.fori_loop(1, n, greet, 0)
    for d in range(1, n_dp):
        pl.semaphore_signal(
            barrier, inc=1, device_id=(lax.rem(dp + d, n_dp), me), device_id_type=MESH
        )
    pl.semaphore_wait(barrier, n - 1 + n_dp - 1)

    def pair(d):
        to = lax.rem(me + d, n)
        where = (dp, to)
        return (
            pltpu.make_async_remote_copy(
                early.at[to], in_e.at[d], send.at[0, d], recv.at[0, d],
                device_id=where, device_id_type=MESH),
            pltpu.make_async_remote_copy(
                late.at[to], in_l.at[d], send.at[1, d], recv.at[1, d],
                device_id=where, device_id_type=MESH),
        )

    def go(d, carry):
        for c in pair(d):
            c.start()
        return carry

    lax.fori_loop(1, n, go, 0)
    mine_e[...] = early[me].astype(F32)
    mine_l[...] = late[me].astype(F32)

    def take(d, carry):
        for c in pair(d):
            c.wait_recv()
        mine_e[...] += in_e[d].astype(F32)
        mine_l[...] += in_l[d].astype(F32)
        return carry

    lax.fori_loop(1, n, take, 0)
    dp_e[0] = mine_e[...].astype(BF)
    dp_l[0] = mine_l[...].astype(BF)
    swaps = []
    for d in range(1, n_dp):
        where = (lax.rem(dp + d, n_dp), me)
        swaps.append(pltpu.make_async_remote_copy(
            dp_e.at[0], dp_e.at[d], dp_send.at[0, d], dp_recv.at[0, d],
            device_id=where, device_id_type=MESH))
        swaps.append(pltpu.make_async_remote_copy(
            dp_l.at[0], dp_l.at[d], dp_send.at[1, d], dp_recv.at[1, d],
            device_id=where, device_id_type=MESH))
    for c in swaps:
        c.start()

    def done(d, carry):
        for c in pair(d):
            c.wait_send()
        return carry

    lax.fori_loop(1, n, done, 0)
    for c in swaps:
        c.wait()
    def total(buf):
        terms = []
        for d in range(n_dp):
            terms.append(buf[d].astype(F32))
        out = jnp.zeros_like(terms[0])
        for source in range(n_dp):
            for d in range(n_dp):
                hit = lax.rem(dp + n_dp - d, n_dp) == source
                out = out + jnp.where(hit, terms[d], 0.0)
        return out

    e = total(dp_e)
    l = total(dp_l)
    o_edge[...] = l[:, :D]
    o_down[...] = l[:, D : D + TW]
    square = jnp.concatenate([e[:, 128 * j : 128 * j + 128] for j in range(8)], axis=0).T
    o_bil[...] = square[:B]
    o_up[...] = e[:, 1024:1152].T


def summed(early, late):
    n = lax.axis_size("graph")
    n_dp = lax.axis_size("dp")
    vm = pl.BlockSpec(memory_space=pltpu.VMEM)
    return pl.pallas_call(
        functools.partial(sum_kernel, n, n_dp),
        out_shape=[
            jax.ShapeDtypeStruct((16, D), F32),
            jax.ShapeDtypeStruct((16, TW), F32),
            jax.ShapeDtypeStruct((B, 128), F32),
            jax.ShapeDtypeStruct((128, 16), F32),
        ],
        in_specs=[vm] * 2,
        out_specs=[vm] * 4,
        scratch_shapes=[
            pltpu.VMEM((n, 16, 1152), BF),
            pltpu.VMEM((n, 16, 640), BF),
            pltpu.VMEM((16, 1152), F32),
            pltpu.VMEM((16, 640), F32),
            pltpu.VMEM((n_dp, 16, 1152), BF),
            pltpu.VMEM((n_dp, 16, 640), BF),
            pltpu.SemaphoreType.DMA((2, n)),
            pltpu.SemaphoreType.DMA((2, n)),
            pltpu.SemaphoreType.DMA((2, n_dp)),
            pltpu.SemaphoreType.DMA((2, n_dp)),
        ],
        compiler_params=pltpu.CompilerParams(
            collective_id=0, has_side_effects=True, vmem_limit_bytes=VMEM_LIMIT
        ),
        name="weight_sums",
    )(early, late)


def body(
    messages, cotangent, triplet_basis, w_edge, w_down, w_bil, w_up,
    trip_src, send_rows, send_count, rev_src, edge_count,
):
    msg, cot = messages[0], cotangent[0]
    factor = 1.0 / math.sqrt(lax.axis_size("dp") * lax.axis_size("graph") * E)
    shifts = offsets(NL)
    idx = trip_src[0].reshape(E // G, G, K).transpose(0, 2, 1).reshape(E // G, T)
    outs = front(msg, cot, w_edge, w_down, send_rows[0], send_count)
    pool, red_send, cot_send = outs[0], outs[1:5], outs[5:9]
    red_recv = [shifted(red_send[o], "graph", shifts[o]) for o in range(NL)]
    cot_recv = [shifted(cot_send[o], "graph", shifts[o]) for o in range(NL)]
    outer, bas, state = fwd(triplet_basis[0], idx, pool, red_recv, w_bil)
    gsx, early = mid(
        factor, state, outer, cot, cot_recv, rev_src.reshape(8, 128), w_up, edge_count
    )
    outs = bwd(gsx, bas, idx, w_bil)
    back = [shifted(outs[1 + o], "graph", -shifts[o]) for o in range(NL)]
    grad_msg, late = tail(
        factor, msg, w_edge, w_down, send_rows[0], send_count, outs[0], back
    )
    g_edge, g_down, g_bil, g_up = summed(early, late)
    return grad_msg[None], g_edge, g_down, g_bil, g_up.reshape(2, TW, 16)


def solution(mesh):
    row = P("dp", "graph", None)
    flat = P("dp", "graph")
    return jax.shard_map(
        body,
        mesh=mesh,
        in_specs=(row, row, row, P(), P(), P(), P(), row, row, flat, flat, flat),
        out_specs=(
            row,
            P("graph", None),
            P("graph", None),
            P(None, "graph"),
            P(None, None, "graph"),
        ),
        check_vma=False,
    )
```

```python
import functools
import math

import jax
import jax.numpy as jnp
from jax import lax
from jax.experimental import pallas as pl
from jax.experimental.pallas import tpu as pltpu
from jax.sharding import PartitionSpec as P

INV_ROOT = 0.7071067811865476
BF = jnp.bfloat16
F32 = jnp.float32
MESH = pl.DeviceIdType.MESH
VMEM_LIMIT = 56 * 1024 * 1024

E = 1024
K = 32
B = 112
TW = 64
D = 512
CAP = 256
NL = 4
G = 8
T = G * K


def offsets(count):
    return [(which // 2 + 1) * (1 - 2 * (which % 2)) for which in range(count)]


def sigmoid(v):
    return 1.0 / (1.0 + jnp.exp(-v))


def silu(v):
    return v * sigmoid(v)


def slope(v):
    s = sigmoid(v)
    return s * (1.0 + v * (1.0 - s))


def iota(shape, dim):
    return lax.broadcasted_iota(jnp.int32, shape, dim)


def dot(a, b):
    return jnp.dot(a, b, preferred_element_type=F32)


def dot_nt(a, b):
    return lax.dot_general(a, b, (((1,), (1,)), ((), ())), preferred_element_type=F32)


def dot_tn(a, b):
    return lax.dot_general(a, b, (((0,), (0,)), ((), ())), preferred_element_type=F32)


def onehot(cond):
    return jnp.where(cond, 1.0, 0.0).astype(BF)


GS = 8
GP = 4
STEPS = E // (G * GS)


def graph_at(distance):
    n = lax.axis_size("graph")
    return (lax.axis_index("dp"), lax.rem(lax.axis_index("graph") + (distance + n), n))


def remote(src, dst, send, recv, where):
    return pltpu.make_async_remote_copy(
        src, dst, send, recv, device_id=where, device_id_type=MESH
    )


def greet(where):
    pl.semaphore_signal(
        pltpu.get_barrier_semaphore(), inc=1, device_id=where, device_id_type=MESH
    )


def load_w(wp, w_bil):
    wp[...] = jnp.zeros_like(wp)
    for ch in range(16):
        wp[128 * ch : 128 * ch + B, :] = w_bil[:, 256 * ch : 256 * ch + 256]


def fold(rows):
    half = rows.shape[0] // 2
    return jnp.concatenate([rows[:half], rows[half:]], axis=1)


def unfold(rows):
    return jnp.concatenate([rows[:, :TW], rows[:, TW:]], axis=0)


def fwd_kernel(msg, cot, w_edge, w_down, rows, count, basis, idx, w_bil, outer, bas, state, cot_out,
               red, pool_t, wp, sbuf, red_send, red_recv, cot_send, cot_recv, send, recv):
    step = pl.program_id(0)
    shifts = offsets(NL)

    def red_copy(o):
        where = graph_at(shifts[o])
        return remote(red_send.at[o], red_recv.at[o], send.at[0, o], recv.at[0, o], where)

    def cot_copy(o):
        where = graph_at(shifts[o])
        return remote(cot_send.at[o], cot_recv.at[o], send.at[1, o], recv.at[1, o], where)

    @pl.when(step == 0)
    def _():
        for o in range(NL):
            greet(graph_at(shifts[o]))
        for i in range(4):
            m = pl.ds(256 * i, 256)
            hidden = silu(dot(msg[m, :], w_edge[...])).astype(BF)
            red[m, :] = silu(dot_nt(hidden, w_down[...])).astype(BF)
        lane = iota((1, CAP), 1)
        lists = []
        for o in range(NL):
            lists.append(jnp.where(lane < count[0, o], rows[o : o + 1, :], -1))
        picks = jnp.concatenate(lists + lists, axis=0).T
        wide = iota((CAP, E), 1)
        for o in range(NL):
            red_send[o] = fold(dot(onehot(wide == picks[:, o : o + 1]), red[...]).astype(BF))
        pl.semaphore_wait(pltpu.get_barrier_semaphore(), NL)
        for o in range(NL):
            red_copy(o).start()
        for o in range(NL):
            cot_send[o] = dot(onehot(wide == picks[:, o : o + 1]), cot[...]).astype(BF)
            cot_copy(o).start()
        load_w(wp, w_bil)
        for hi in range(8):
            if hi < 4:
                src = fold(red[256 * hi : 256 * hi + 256, :])
            else:
                red_copy(hi - 4).wait_recv()
                src = red_recv[hi - 4]
            flip = src.astype(F32).T
            pool_t[64 * hi : 64 * hi + 64, :] = jnp.concatenate(
                [flip[:64], flip[64:]], axis=1
            ).astype(BF)

    @pl.when(step == STEPS - 1)
    def _():
        for o in range(NL):
            red_copy(o).wait_send()
            cot_copy(o).wait()
        cot_out[...] = cot_recv[...]

    e_lane = lax.rem(iota((16, T), 1), G)
    quad = iota((16, T), 0) // 4
    keep = [onehot(e_lane == 4 * q + quad) for q in range(2)]
    low = iota((8, T), 0) < 4

    def some(j, carry):
        hots, his = [], []
        for i in range(GP):
            row = idx[pl.ds(j * GP + i, 1), :]
            hots.append(onehot(iota((256, T), 0) == jnp.bitwise_and(row, 255)))
            his.append(jnp.right_shift(row, 8))
        found = dot(pool_t[...], jnp.concatenate(hots, axis=1))
        for i in range(GP):
            g = j * GP + i
            wide = basis[pl.ds(pl.multiple_of(g * G, G), G), :].astype(F32)
            pieces = []
            for k in range(K):
                piece = wide[:, k * B : (k + 1) * B]
                pieces.append(jnp.concatenate([piece, jnp.zeros((G, 128 - B), F32)], axis=1))
            rhs = jnp.concatenate(pieces, axis=0).astype(BF)
            bas[pl.ds(pl.multiple_of(g * T, T), T), :] = rhs
            got = jnp.zeros((TW, T), F32)
            for hi in range(8):
                part = found[64 * hi : 64 * hi + 64, T * i : T * i + T]
                got = jnp.where(his[i] == hi, part, got)
            tiles = []
            for v in range(8):
                x = got[8 * v : 8 * v + 8]
                y = pltpu.roll(x, 4, 0)
                for d in (jnp.where(low, x, y), jnp.where(low, y, x)):
                    tiles.append(jnp.concatenate([d, d], axis=0).astype(BF))
            lhs = jnp.concatenate([t * keep[q] for q in range(2) for t in tiles], axis=0)
            out = dot(lhs, rhs).astype(BF)
            for q in range(2):
                for ch in range(16):
                    at = (q * 16 + ch) * 16
                    outer[pl.ds(pl.multiple_of(g * 32 + 16 * q, 16), 16), 128 * ch : 128 * ch + 128] = (
                        out[at : at + 16]
                    )
        return carry

    lax.fori_loop(0, GS // GP, some, 0)
    rows = 32 * GS
    full = dot(outer[...], wp[...])
    full = jnp.where(lax.rem(iota((rows, 256), 0), 4) == iota((rows, 256), 1) // 64, full, 0.0)
    full = full + pltpu.roll(full, 1, 0)
    full = full + pltpu.roll(full, 2, 0)
    sbuf[...] = full[:, :128] + full[:, 128:]
    picked = sbuf[pl.ds(3, G * GS, stride=4), :]
    state[...] = (picked + pltpu.roll(picked, 64, 1)).astype(BF)


def fwd(msg, cot, w_edge, w_down, rows, count, basis, idx, w_bil):
    whole = lambda shape: pl.BlockSpec(shape, lambda i: (0,) * len(shape))
    return pl.pallas_call(
        fwd_kernel,
        grid=(STEPS,),
        out_shape=[
            jax.ShapeDtypeStruct((4 * E, 2048), BF),
            jax.ShapeDtypeStruct((E * K, 128), BF),
            jax.ShapeDtypeStruct((E, 128), BF),
            jax.ShapeDtypeStruct((NL, CAP, D), BF),
        ],
        in_specs=[
            whole((E, D)), whole((E, D)), whole((D, D)), whole((TW, D)), whole((NL, CAP)),
            pl.BlockSpec(memory_space=pltpu.SMEM),
            pl.BlockSpec((G * GS, K * B), lambda i: (i, 0)),
            pl.BlockSpec((GS, T), lambda i: (i, 0)),
            whole((B, 4096)),
        ],
        out_specs=[
            pl.BlockSpec((32 * GS, 2048), lambda i: (i, 0)),
            pl.BlockSpec((T * GS, 128), lambda i: (i, 0)),
            pl.BlockSpec((G * GS, 128), lambda i: (i, 0)),
            whole((NL, CAP, D)),
        ],
        scratch_shapes=[
            pltpu.VMEM((E, TW), BF),
            pltpu.VMEM((512, 256), BF),
            pltpu.VMEM((2048, 256), BF),
            pltpu.VMEM((32 * GS, 128), F32),
            pltpu.VMEM((NL, 128, 128), BF),
            pltpu.VMEM((NL, 128, 128), BF),
            pltpu.VMEM((NL, CAP, D), BF),
            pltpu.VMEM((NL, CAP, D), BF),
            pltpu.SemaphoreType.DMA((2, NL)),
            pltpu.SemaphoreType.DMA((2, NL)),
        ],
        compiler_params=pltpu.CompilerParams(
            collective_id=0, has_side_effects=True, vmem_limit_bytes=VMEM_LIMIT
        ),
        name="triplets_out",
    )(msg, cot, w_edge, w_down, rows, count, basis, idx, w_bil)


BE = 128


def mid_kernel(factor, state, outer, cot, all_cot, far_cot, rev, w_up, count, gsx, early, bil, up):
    step = pl.program_id(0)

    @pl.when(step == 0)
    def _():
        bil[...] = jnp.zeros_like(bil)
        up[...] = jnp.zeros_like(up)

    st = state[...][:, :TW]
    alive = iota((BE, D), 0) + step * BE < count[0, 0]
    scaled = jnp.where(alive, cot[...].astype(F32) * INV_ROOT, 0.0)
    grad_ca = (scaled * slope(dot(st, w_up[0]))).astype(BF)
    row = rev[pl.ds(step, 1), :]
    col = jnp.concatenate([row] * 8, axis=0).T[:, :1]
    mirror = dot(onehot(iota((BE, E), 1) == col), all_cot[...])
    mirror = mirror + dot(onehot(iota((BE, NL * CAP), 1) + E == col), far_cot[...])
    grad_ac = (mirror * INV_ROOT * slope(dot(st, w_up[1]))).astype(BF)
    up[:TW, :] += dot_tn(st, grad_ca)
    up[TW:, :] += dot_tn(st, grad_ac)
    own = dot_nt(grad_ca, jnp.concatenate([w_up[0]] * 4, axis=0))
    back = dot_nt(grad_ac, jnp.concatenate([w_up[1]] * 4, axis=0)).astype(BF)
    grad_state = (own + back.astype(F32)).astype(BF)
    spread = onehot(iota((4 * BE, BE), 0) // 4 == iota((4 * BE, BE), 1))
    big = dot(spread, grad_state)
    big = jnp.where(lax.rem(iota((4 * BE, 256), 0), 4) == iota((4 * BE, 256), 1) // 64, big, 0.0)
    big = big.astype(BF)
    gsx[...] = big
    bil[...] += dot_tn(big, outer[...])

    @pl.when(step == pl.num_programs(0) - 1)
    def _():
        turned = (up[...] * factor).T.astype(BF)
        for i in range(32):
            early[i, :, 1024:1152] = turned[16 * i : 16 * i + 16]
            r, c = (i % 2) * 128, (i // 2) * 128
            for j in range(8):
                early[i, :, 128 * j : 128 * j + 128] = (
                    bil[r + 16 * j : r + 16 * j + 16, c : c + 128] * factor
                ).astype(BF)


def mid(factor, state, outer, cot, recv, rev, w_up, count):
    whole = lambda shape: pl.BlockSpec(shape, lambda i: (0,) * len(shape))
    return pl.pallas_call(
        functools.partial(mid_kernel, factor),
        grid=(E // BE,),
        out_shape=[
            jax.ShapeDtypeStruct((4 * E, 256), BF),
            jax.ShapeDtypeStruct((32, 16, 1152), BF),
        ],
        in_specs=[
            pl.BlockSpec((BE, 128), lambda i: (i, 0)),
            pl.BlockSpec((4 * BE, 2048), lambda i: (i, 0)),
            pl.BlockSpec((BE, D), lambda i: (i, 0)),
            whole((E, D)),
            whole((NL * CAP, D)),
        ]
        + [whole((8, 128)), whole((2, TW, D)), pl.BlockSpec(memory_space=pltpu.SMEM)],
        out_specs=[
            pl.BlockSpec((4 * BE, 256), lambda i: (i, 0)),
            whole((32, 16, 1152)),
        ],
        scratch_shapes=[pltpu.VMEM((256, 2048), F32), pltpu.VMEM((2 * TW, D), F32)],
        compiler_params=pltpu.CompilerParams(vmem_limit_bytes=VMEM_LIMIT),
        name="middle",
    )(state, outer, cot, cot, recv, rev, w_up, count)


SWAP = 10


def bwd_kernel(factor, n, n_dp, gsx, bas, idx, w_bil, early, msg, w_edge, w_down, rows, count,
               grad_msg, sum_e, sum_l, wp, go, acc, ret_send, ret_recv, s_edge, hid, s_down, gedge,
               late, in_e, pair_in, pair_out, in_l, dp_e, dp_l,
               e_send, e_recv, l_send, l_recv, r_send, r_recv, p_send, p_recv, d_send, d_recv):
    step = pl.program_id(0)
    shifts = offsets(NL)
    me = lax.axis_index("graph")
    dp = lax.axis_index("dp")
    core = lax.rem(me, 2)
    chip = me // 2
    chips = n // 2

    def early_copy(d):
        to = lax.rem(me + d, n)
        return remote(early.at[to], in_e.at[d], e_send.at[d], e_recv.at[d], (dp, to))

    def late_copy(d):
        to = lax.rem(chip + d, chips)
        return remote(pair_out.at[to], in_l.at[d], l_send.at[d], l_recv.at[d], (dp, 2 * to + core))

    def swap(which, buf):
        out = []
        for d in range(1, n_dp):
            where = (lax.rem(dp + d, n_dp), me)
            out.append(remote(buf.at[0], buf.at[d], d_send.at[which, d], d_recv.at[which, d], where))
        return out

    def total(buf):
        terms = [buf[d].astype(F32) for d in range(n_dp)]
        out = jnp.zeros_like(terms[0])
        for source in range(n_dp):
            for d in range(n_dp):
                hit = lax.rem(dp + (n_dp - d), n_dp) == source
                out = out + jnp.where(hit, terms[d], 0.0)
        return out

    @pl.when(step == 0)
    def _():
        def hello(d, carry):
            greet((dp, lax.rem(me + d, n)))
            return carry

        lax.fori_loop(1, n, hello, 0)
        for d in range(1, n_dp):
            greet((lax.rem(dp + d, n_dp), me))
        load_w(wp, w_bil)
        acc[...] = jnp.zeros_like(acc)
        pl.semaphore_wait(pltpu.get_barrier_semaphore(), n - 1 + n_dp - 1)

        def begin(d, carry):
            early_copy(d).start()
            return carry

        lax.fori_loop(1, n, begin, 0)

    @pl.when(step == SWAP)
    def _():
        def take(d, total_):
            early_copy(d).wait()
            return total_ + in_e[d].astype(F32)

        dp_e[0] = lax.fori_loop(1, n, take, early[me].astype(F32)).astype(BF)
        for c in swap(0, dp_e):
            c.start()

    go[...] = dot_nt(gsx[...], wp[...]).astype(BF)
    e_lane = lax.rem(iota((8, T), 1), G)
    pair = e_lane // 2
    odd = lax.rem(e_lane, 2) == 1
    stay = (iota((8, T), 0) >= 4) == odd

    def some(j, carry):
        hots, sides = [], []
        for i in range(GP):
            g = j * GP + i
            row = idx[pl.ds(g, 1), :]
            hots.append(onehot(iota((256, T), 0) == jnp.bitwise_and(row, 255)))
            hi_of = jnp.right_shift(row, 8)
            lhs = jnp.concatenate(
                [
                    go[pl.ds(pl.multiple_of(g * 32 + 16 * q, 16), 16), 128 * ch : 128 * ch + 128]
                    for q in range(2)
                    for ch in range(16)
                ],
                axis=0,
            )
            full = dot_nt(lhs, bas[pl.ds(pl.multiple_of(g * T, T), T), :])
            picked = []
            for ch in range(16):
                z = full[16 * ch : 16 * ch + 8]
                for p in range(1, 4):
                    at = (p // 2) * 256 + 16 * ch + 8 * (p % 2)
                    z = jnp.where(pair == p, full[at : at + 8], z)
                picked.append(z)
            grads = []
            for v in range(8):
                z0, z1 = picked[2 * v], picked[2 * v + 1]
                here = jnp.where(odd, z1, z0)
                there = jnp.where(odd, z0, z1)
                grads.append(jnp.where(stay, here, pltpu.roll(there, 4, 0)))
            grad = jnp.concatenate(grads, axis=0).astype(BF)
            sides.append(
                jnp.concatenate([grad * onehot(hi_of == hi) for hi in range(8)], axis=0)
            )
        acc[...] += dot_nt(jnp.concatenate(sides, axis=1), jnp.concatenate(hots, axis=1))
        return carry

    lax.fori_loop(0, GS // GP, some, 0)

    @pl.when(step == pl.num_programs(0) - 1)
    def _():
        def back(o):
            return remote(ret_send.at[o], ret_recv.at[o], r_send.at[o], r_recv.at[o], graph_at(-shifts[o]))

        for o in range(NL):
            part = acc[64 * (4 + o) : 64 * (4 + o) + 64, :]
            ret_send[o] = jnp.concatenate([part[:, :128], part[:, 128:]], axis=0).T.astype(BF)
            back(o).start()
        for i in range(4):
            m = pl.ds(256 * i, 256)
            pre_edge = dot(msg[m, :], w_edge[...])
            s_edge[m, :] = slope(pre_edge)
            hidden = silu(pre_edge).astype(BF)
            hid[m, :] = hidden
            s_down[m, :] = slope(dot_nt(hidden, w_down[...]))
        hots, backs = [], []
        for o in range(NL):
            picks = jnp.where(iota((1, CAP), 1) < count[0, o], rows[o : o + 1, :], -1)
            hots.append(onehot(iota((E, CAP), 0) == picks))
        for o in range(NL):
            back(o).wait()
            backs.append(unfold(ret_recv[o]))
        far = dot(jnp.concatenate(hots, axis=1), jnp.concatenate(backs, axis=0))
        downs = jnp.zeros((D, TW), F32)
        for i in range(4):
            m = pl.ds(256 * i, 256)
            part = acc[64 * i : 64 * i + 64, :]
            own = jnp.concatenate([part[:, :128], part[:, 128:]], axis=0).T
            grad_down = ((far[256 * i : 256 * i + 256] + unfold(own)) * s_down[m, :]).astype(BF)
            downs = downs + dot_tn(hid[m, :], grad_down)
            gedge[m, :] = (dot(grad_down, w_down[...]) * s_edge[m, :]).astype(BF)
        edges = dot_tn(msg[...], gedge[...])
        both = jnp.concatenate(
            [edges * factor, downs * factor, jnp.zeros((D, TW), F32)], axis=1
        ).astype(BF)
        for i in range(n):
            late[i % 2, i // 2] = both[16 * i : 16 * i + 16]
        sibling = (dp, me + 1 - 2 * core)
        first = remote(late.at[1 - core], pair_in, p_send, p_recv, sibling)
        first.start()
        for i in range(4):
            m = pl.ds(256 * i, 256)
            grad_msg[m, :] = dot_nt(gedge[m, :], w_edge[...]).astype(BF)
        first.wait()
        pair_out[...] = (late[core].astype(F32) + pair_in[...].astype(F32)).astype(BF)

        def begin(d, carry):
            late_copy(d).start()
            return carry

        lax.fori_loop(1, chips, begin, 0)
        for c in swap(0, dp_e):
            c.wait()
        sum_e[...] = total(dp_e)

        def take(d, total_):
            late_copy(d).wait()
            return total_ + in_l[d].astype(F32)

        dp_l[0] = lax.fori_loop(1, chips, take, pair_out[chip].astype(F32)).astype(BF)
        for c in swap(1, dp_l):
            c.start()
        for c in swap(1, dp_l):
            c.wait()
        sum_l[...] = total(dp_l)


def bwd(factor, gsx, bas, idx, w_bil, early, msg, w_edge, w_down, rows, count):
    whole = lambda shape: pl.BlockSpec(shape, lambda i: (0,) * len(shape))
    n = lax.axis_size("graph")
    n_dp = lax.axis_size("dp")
    dma = pltpu.SemaphoreType.DMA
    return pl.pallas_call(
        functools.partial(bwd_kernel, factor, n, n_dp),
        grid=(STEPS,),
        out_shape=[
            jax.ShapeDtypeStruct((E, D), BF),
            jax.ShapeDtypeStruct((16, 1152), F32),
            jax.ShapeDtypeStruct((16, 640), F32),
        ],
        in_specs=[
            pl.BlockSpec((32 * GS, 256), lambda i: (i, 0)),
            pl.BlockSpec((T * GS, 128), lambda i: (i, 0)),
            pl.BlockSpec((GS, T), lambda i: (i, 0)),
            whole((B, 4096)), whole((n, 16, 1152)),
            whole((E, D)), whole((D, D)), whole((TW, D)), whole((NL, CAP)),
            pl.BlockSpec(memory_space=pltpu.SMEM),
        ],
        out_specs=[whole((E, D)), whole((16, 1152)), whole((16, 640))],
        scratch_shapes=[
            pltpu.VMEM((2048, 256), BF),
            pltpu.VMEM((32 * GS, 2048), BF),
            pltpu.VMEM((512, 256), F32),
            pltpu.VMEM((NL, 128, 128), BF),
            pltpu.VMEM((NL, 128, 128), BF),
            pltpu.VMEM((E, D), F32),
            pltpu.VMEM((E, D), BF),
            pltpu.VMEM((E, TW), F32),
            pltpu.VMEM((E, D), BF),
            pltpu.VMEM((2, n // 2, 16, 640), BF),
            pltpu.VMEM((n, 16, 1152), BF),
            pltpu.VMEM((n // 2, 16, 640), BF),
            pltpu.VMEM((n // 2, 16, 640), BF),
            pltpu.VMEM((n // 2, 16, 640), BF),
            pltpu.VMEM((n_dp, 16, 1152), BF),
            pltpu.VMEM((n_dp, 16, 640), BF),
            dma((n,)), dma((n,)), dma((n // 2,)), dma((n // 2,)), dma((NL,)), dma((NL,)),
            dma, dma, dma((2, n_dp)), dma((2, n_dp)),
        ],
        compiler_params=pltpu.CompilerParams(
            collective_id=1, has_side_effects=True, vmem_limit_bytes=VMEM_LIMIT
        ),
        name="triplets_back",
    )(gsx, bas, idx, w_bil, early, msg, w_edge, w_down, rows, count)


def last_kernel(grad_msg, e, l, o_msg, o_edge, o_down, o_bil, o_up, sem):
    move = pltpu.make_async_copy(grad_msg, o_msg, sem)
    move.start()
    o_edge[...] = l[:, :D]
    o_down[...] = l[:, D : D + TW]
    square = jnp.concatenate([e[:, 128 * j : 128 * j + 128] for j in range(8)], axis=0).T
    o_bil[...] = square[:B]
    o_up[0] = e[:, 1024:1088]
    o_up[1] = e[:, 1088:1152]
    move.wait()


def last(grad_msg, e, l):
    vm = pl.BlockSpec(memory_space=pltpu.VMEM)
    hbm = pl.BlockSpec(memory_space=pl.ANY)
    return pl.pallas_call(
        last_kernel,
        out_shape=[
            jax.ShapeDtypeStruct((E, D), BF),
            jax.ShapeDtypeStruct((16, D), F32),
            jax.ShapeDtypeStruct((16, TW), F32),
            jax.ShapeDtypeStruct((B, 128), F32),
            jax.ShapeDtypeStruct((2, 16, TW), F32),
        ],
        in_specs=[hbm, vm, vm],
        out_specs=[hbm, vm, vm, vm, vm],
        scratch_shapes=[pltpu.SemaphoreType.DMA],
        name="outputs",
    )(grad_msg, e, l)


def body(
    messages, cotangent, triplet_basis, w_edge, w_down, w_bil, w_up,
    trip_src, send_rows, send_count, rev_src, edge_count,
):
    msg, cot = messages[0], cotangent[0]
    narrow = w_down.T
    rows = send_rows[0]
    factor = 1.0 / math.sqrt(lax.axis_size("dp") * lax.axis_size("graph") * E)
    idx = trip_src[0].reshape(E // G, G, K).transpose(0, 2, 1).reshape(E // G, T)
    outer, bas, state, far = fwd(
        msg, cot, w_edge, narrow, rows, send_count, triplet_basis[0], idx, w_bil
    )
    gsx, early = mid(
        factor, state, outer, cot, far.reshape(NL * CAP, D), rev_src.reshape(8, 128), w_up, edge_count
    )
    grad_msg, e, l = bwd(factor, gsx, bas, idx, w_bil, early, msg, w_edge, narrow, rows, send_count)
    grad_msg, g_edge, g_down, g_bil, g_up = last(grad_msg, e, l)
    return grad_msg[None], g_edge, g_down, g_bil, g_up.transpose(0, 2, 1)


def solution(mesh):
    row = P("dp", "graph", None)
    flat = P("dp", "graph")
    return jax.shard_map(
        body,
        mesh=mesh,
        in_specs=(row, row, row, P(), P(), P(), P(), row, row, flat, flat, flat),
        out_specs=(
            row,
            P("graph", None),
            P("graph", None),
            P(None, "graph"),
            P(None, None, "graph"),
        ),
        check_vma=False,
    )
```

```python
import functools
import math

import jax
import jax.numpy as jnp
from jax import lax
from jax.experimental import pallas as pl
from jax.experimental.pallas import tpu as pltpu
from jax.sharding import PartitionSpec as P

INV_ROOT = 0.7071067811865476
BF = jnp.bfloat16
F32 = jnp.float32
MESH = pl.DeviceIdType.MESH
VMEM_LIMIT = 56 * 1024 * 1024

E = 1024
K = 32
B = 112
TW = 64
D = 512
CAP = 256
NL = 4
G = 8
T = G * K


def offsets(count):
    return [(which // 2 + 1) * (1 - 2 * (which % 2)) for which in range(count)]


def sigmoid(v):
    return 0.5 + 0.5 * jnp.tanh(0.5 * v)


def silu(v):
    return v * sigmoid(v)


def slope(v):
    s = sigmoid(v)
    return s * (1.0 + v * (1.0 - s))


def iota(shape, dim):
    return lax.broadcasted_iota(jnp.int32, shape, dim)


def dot(a, b):
    return jnp.dot(a, b, preferred_element_type=F32)


def dot_nt(a, b):
    return lax.dot_general(a, b, (((1,), (1,)), ((), ())), preferred_element_type=F32)


def dot_tn(a, b):
    return lax.dot_general(a, b, (((0,), (0,)), ((), ())), preferred_element_type=F32)


def onehot(cond):
    return jnp.where(cond, 1.0, 0.0).astype(BF)


GS = 16
GP = 4
STEPS = E // (G * GS)


def graph_at(distance):
    n = lax.axis_size("graph")
    return (lax.axis_index("dp"), lax.rem(lax.axis_index("graph") + (distance + n), n))


def remote(src, dst, send, recv, where):
    return pltpu.make_async_remote_copy(
        src, dst, send, recv, device_id=where, device_id_type=MESH
    )


def greet(where):
    pl.semaphore_signal(
        pltpu.get_barrier_semaphore(), inc=1, device_id=where, device_id_type=MESH
    )


def load_w(wp, w_bil):
    wp[...] = jnp.zeros_like(wp)
    for ch in range(16):
        wp[128 * ch : 128 * ch + B, :] = w_bil[:, 256 * ch : 256 * ch + 256]


def fold(rows):
    half = rows.shape[0] // 2
    return jnp.concatenate([rows[:half], rows[half:]], axis=1)


def unfold(rows):
    return jnp.concatenate([rows[:, :TW], rows[:, TW:]], axis=0)


def fwd_kernel(msg, cot, w_edge, w_down, rows, count, basis, idx, w_bil, outer, bas, state, cot_out,
               red, pool_t, wp, sbuf, red_send, red_recv, cot_send, cot_recv, send, recv):
    step = pl.program_id(0)
    shifts = offsets(NL)

    def red_copy(o):
        where = graph_at(shifts[o])
        return remote(red_send.at[o], red_recv.at[o], send.at[0, o], recv.at[0, o], where)

    def cot_copy(o):
        where = graph_at(shifts[o])
        return remote(cot_send.at[o], cot_recv.at[o], send.at[1, o], recv.at[1, o], where)

    @pl.when(step == 0)
    def _():
        for o in range(NL):
            greet(graph_at(shifts[o]))
        for i in range(4):
            m = pl.ds(256 * i, 256)
            hidden = silu(dot(msg[m, :], w_edge[...])).astype(BF)
            red[m, :] = silu(dot_nt(hidden, w_down[...])).astype(BF)
        lane = iota((1, CAP), 1)
        lists = []
        for o in range(NL):
            lists.append(jnp.where(lane < count[0, o], rows[o : o + 1, :], -1))
        picks = jnp.concatenate(lists + lists, axis=0).T
        wide = iota((CAP, E), 1)
        for o in range(NL):
            red_send[o] = fold(dot(onehot(wide == picks[:, o : o + 1]), red[...]).astype(BF))
        pl.semaphore_wait(pltpu.get_barrier_semaphore(), NL)
        for o in range(NL):
            red_copy(o).start()
        for o in range(NL):
            cot_send[o] = dot(onehot(wide == picks[:, o : o + 1]), cot[...]).astype(BF)
            cot_copy(o).start()
        load_w(wp, w_bil)
        for hi in range(8):
            if hi < 4:
                src = fold(red[256 * hi : 256 * hi + 256, :])
            else:
                red_copy(hi - 4).wait_recv()
                src = red_recv[hi - 4]
            flip = src.astype(F32).T
            pool_t[64 * hi : 64 * hi + 64, :] = jnp.concatenate(
                [flip[:64], flip[64:]], axis=1
            ).astype(BF)

    @pl.when(step == STEPS - 1)
    def _():
        for o in range(NL):
            red_copy(o).wait_send()
            cot_copy(o).wait()
        cot_out[...] = cot_recv[...]

    keep = onehot(lax.rem(iota((16, T), 1), 4) == iota((16, T), 0) // 4)
    low = iota((8, T), 0) < 4
    low1 = iota((8, 128), 0) < 4

    def some(j, carry):
        hots, his = [], []
        for i in range(GP):
            row = idx[pl.ds(j * GP + i, 1), :]
            hots.append(onehot(iota((256, T), 0) == jnp.bitwise_and(row, 255)))
            his.append(jnp.right_shift(row, 8))
        found = dot(pool_t[...], jnp.concatenate(hots, axis=1)).astype(BF)
        founds = [found[:, T * i : T * i + T] for i in range(GP)]
        for i in range(GP):
            g = j * GP + i
            wide = basis[pl.ds(pl.multiple_of(g * G, G), G), :].astype(F32)
            pieces = []
            for k in range(K):
                piece = wide[:, k * B : (k + 1) * B]
                pieces.append(jnp.concatenate([piece, jnp.zeros((G, 128 - B), F32)], axis=1))
            first, second = [], []
            for k in range(0, K, 2):
                x, y = pieces[k], pieces[k + 1]
                z = pltpu.roll(jnp.where(low1, y, x), 4, 0)
                first.append(jnp.where(low1, x, z))
                second.append(jnp.where(low1, z, y))
            first = jnp.concatenate(first, axis=0).astype(BF)
            second = jnp.concatenate(second, axis=0).astype(BF)
            zero = jnp.zeros((128, 128), BF)
            at = pl.multiple_of(g * T, T)
            bas[pl.ds(at, 128), :] = first
            bas[pl.ds(at + 128, 128), :] = second
            rhs = jnp.concatenate(
                [jnp.concatenate([first, zero], axis=1), jnp.concatenate([zero, second], axis=1)], axis=0
            )
            got = founds[i][:64] * onehot(his[i] == 0)
            for hi in range(1, 8):
                got = got + founds[i][64 * hi : 64 * hi + 64] * onehot(his[i] == hi)
            got = got.astype(F32)
            tiles = []
            for v in range(8):
                x = got[8 * v : 8 * v + 8]
                y = pltpu.roll(x, 4, 0)
                for d in (jnp.where(low, x, y), jnp.where(low, y, x)):
                    tiles.append(jnp.concatenate([d, d], axis=0).astype(BF) * keep)
            lhs = jnp.concatenate(tiles, axis=0)
            out = dot(lhs, rhs).astype(BF)
            for q in range(2):
                for ch in range(16):
                    outer[pl.ds(pl.multiple_of(g * 32 + 16 * q, 16), 16), 128 * ch : 128 * ch + 128] = (
                        out[16 * ch : 16 * ch + 16, 128 * q : 128 * q + 128]
                    )
        return carry

    lax.fori_loop(0, GS // GP, some, 0)
    rows = 32 * GS
    full = dot(outer[...], wp[...])
    full = jnp.where(lax.rem(iota((rows, 256), 0), 4) == iota((rows, 256), 1) // 64, full, 0.0)
    full = full + pltpu.roll(full, 1, 0)
    full = full + pltpu.roll(full, 2, 0)
    sbuf[...] = full[:, :128] + full[:, 128:]
    picked = sbuf[pl.ds(3, G * GS, stride=4), :]
    state[...] = (picked + pltpu.roll(picked, 64, 1)).astype(BF)


def fwd(msg, cot, w_edge, w_down, rows, count, basis, idx, w_bil):
    whole = lambda shape: pl.BlockSpec(shape, lambda i: (0,) * len(shape))
    return pl.pallas_call(
        fwd_kernel,
        grid=(STEPS,),
        out_shape=[
            jax.ShapeDtypeStruct((4 * E, 2048), BF),
            jax.ShapeDtypeStruct((E * K, 128), BF),
            jax.ShapeDtypeStruct((E, 128), BF),
            jax.ShapeDtypeStruct((NL, CAP, D), BF),
        ],
        in_specs=[
            whole((E, D)), whole((E, D)), whole((D, D)), whole((TW, D)), whole((NL, CAP)),
            pl.BlockSpec(memory_space=pltpu.SMEM),
            pl.BlockSpec((G * GS, K * B), lambda i: (i, 0)),
            pl.BlockSpec((GS, T), lambda i: (i, 0)),
            whole((B, 4096)),
        ],
        out_specs=[
            pl.BlockSpec((32 * GS, 2048), lambda i: (i, 0)),
            pl.BlockSpec((T * GS, 128), lambda i: (i, 0)),
            pl.BlockSpec((G * GS, 128), lambda i: (i, 0)),
            whole((NL, CAP, D)),
        ],
        scratch_shapes=[
            pltpu.VMEM((E, TW), BF),
            pltpu.VMEM((512, 256), BF),
            pltpu.VMEM((2048, 256), BF),
            pltpu.VMEM((32 * GS, 128), F32),
            pltpu.VMEM((NL, 128, 128), BF),
            pltpu.VMEM((NL, 128, 128), BF),
            pltpu.VMEM((NL, CAP, D), BF),
            pltpu.VMEM((NL, CAP, D), BF),
            pltpu.SemaphoreType.DMA((2, NL)),
            pltpu.SemaphoreType.DMA((2, NL)),
        ],
        compiler_params=pltpu.CompilerParams(
            collective_id=0, has_side_effects=True, vmem_limit_bytes=VMEM_LIMIT
        ),
        name="triplets_out",
    )(msg, cot, w_edge, w_down, rows, count, basis, idx, w_bil)


BE = 128


def mid_kernel(factor, state, outer, cot, all_cot, far_cot, rev, w_up, count, gsx, early, bil, up):
    step = pl.program_id(0)

    @pl.when(step == 0)
    def _():
        bil[...] = jnp.zeros_like(bil)
        up[...] = jnp.zeros_like(up)

    st = state[...][:, :TW]
    alive = iota((BE, D), 0) + step * BE < count[0, 0]
    scaled = jnp.where(alive, cot[...].astype(F32) * INV_ROOT, 0.0)
    grad_ca = (scaled * slope(dot(st, w_up[0]))).astype(BF)
    row = rev[pl.ds(step, 1), :]
    col = jnp.concatenate([row] * 8, axis=0).T[:, :1]
    mirror = dot(onehot(iota((BE, E), 1) == col), all_cot[...])
    mirror = mirror + dot(onehot(iota((BE, NL * CAP), 1) + E == col), far_cot[...])
    grad_ac = (mirror * INV_ROOT * slope(dot(st, w_up[1]))).astype(BF)
    up[:TW, :] += dot_tn(st, grad_ca)
    up[TW:, :] += dot_tn(st, grad_ac)
    own = dot_nt(grad_ca, jnp.concatenate([w_up[0]] * 4, axis=0))
    back = dot_nt(grad_ac, jnp.concatenate([w_up[1]] * 4, axis=0)).astype(BF)
    grad_state = (own + back.astype(F32)).astype(BF)
    spread = onehot(iota((4 * BE, BE), 0) // 4 == iota((4 * BE, BE), 1))
    big = dot(spread, grad_state)
    big = jnp.where(lax.rem(iota((4 * BE, 256), 0), 4) == iota((4 * BE, 256), 1) // 64, big, 0.0)
    big = big.astype(BF)
    gsx[...] = big
    bil[...] += dot_tn(big, outer[...])

    @pl.when(step == pl.num_programs(0) - 1)
    def _():
        turned = (up[...] * factor).T.astype(BF)
        for i in range(32):
            early[i, :, 1024:1152] = turned[16 * i : 16 * i + 16]
            r, c = (i % 2) * 128, (i // 2) * 128
            for j in range(8):
                early[i, :, 128 * j : 128 * j + 128] = (
                    bil[r + 16 * j : r + 16 * j + 16, c : c + 128] * factor
                ).astype(BF)


def mid(factor, state, outer, cot, recv, rev, w_up, count):
    whole = lambda shape: pl.BlockSpec(shape, lambda i: (0,) * len(shape))
    return pl.pallas_call(
        functools.partial(mid_kernel, factor),
        grid=(E // BE,),
        out_shape=[
            jax.ShapeDtypeStruct((4 * E, 256), BF),
            jax.ShapeDtypeStruct((32, 16, 1152), BF),
        ],
        in_specs=[
            pl.BlockSpec((BE, 128), lambda i: (i, 0)),
            pl.BlockSpec((4 * BE, 2048), lambda i: (i, 0)),
            pl.BlockSpec((BE, D), lambda i: (i, 0)),
            whole((E, D)),
            whole((NL * CAP, D)),
        ]
        + [whole((8, 128)), whole((2, TW, D)), pl.BlockSpec(memory_space=pltpu.SMEM)],
        out_specs=[
            pl.BlockSpec((4 * BE, 256), lambda i: (i, 0)),
            whole((32, 16, 1152)),
        ],
        scratch_shapes=[pltpu.VMEM((256, 2048), F32), pltpu.VMEM((2 * TW, D), F32)],
        compiler_params=pltpu.CompilerParams(vmem_limit_bytes=VMEM_LIMIT),
        name="middle",
    )(state, outer, cot, cot, recv, rev, w_up, count)


SWAP = 5


def bwd_kernel(factor, n, n_dp, gsx, bas, idx, w_bil, early, msg, w_edge, w_down, rows, count,
               grad_msg, sum_e, sum_l, wp, go, acc, ret_send, ret_recv, s_edge, hid, s_down, gedge,
               late, in_e, pair_in, pair_out, in_l, dp_e, dp_l,
               e_send, e_recv, l_send, l_recv, r_send, r_recv, p_send, p_recv, d_send, d_recv):
    step = pl.program_id(0)
    shifts = offsets(NL)
    me = lax.axis_index("graph")
    dp = lax.axis_index("dp")
    core = lax.rem(me, 2)
    chip = me // 2
    chips = n // 2

    def early_copy(d):
        to = lax.rem(me + d, n)
        return remote(early.at[to], in_e.at[d], e_send.at[d], e_recv.at[d], (dp, to))

    def late_copy(d):
        to = lax.rem(chip + d, chips)
        return remote(pair_out.at[to], in_l.at[d], l_send.at[d], l_recv.at[d], (dp, 2 * to + core))

    def swap(which, buf):
        out = []
        for d in range(1, n_dp):
            where = (lax.rem(dp + d, n_dp), me)
            out.append(remote(buf.at[0], buf.at[d], d_send.at[which, d], d_recv.at[which, d], where))
        return out

    def total(buf):
        terms = [buf[d].astype(F32) for d in range(n_dp)]
        out = jnp.zeros_like(terms[0])
        for source in range(n_dp):
            for d in range(n_dp):
                hit = lax.rem(dp + (n_dp - d), n_dp) == source
                out = out + jnp.where(hit, terms[d], 0.0)
        return out

    @pl.when(step == 0)
    def _():
        def hello(d, carry):
            greet((dp, lax.rem(me + d, n)))
            return carry

        lax.fori_loop(1, n, hello, 0)
        for d in range(1, n_dp):
            greet((lax.rem(dp + d, n_dp), me))
        load_w(wp, w_bil)
        acc[...] = jnp.zeros_like(acc)
        pl.semaphore_wait(pltpu.get_barrier_semaphore(), n - 1 + n_dp - 1)

        def begin(d, carry):
            early_copy(d).start()
            return carry

        lax.fori_loop(1, n, begin, 0)

    @pl.when(step == SWAP)
    def _():
        def take(d, total_):
            early_copy(d).wait()
            return total_ + in_e[d].astype(F32)

        dp_e[0] = lax.fori_loop(1, n, take, early[me].astype(F32)).astype(BF)
        for c in swap(0, dp_e):
            c.start()

    go[...] = dot_nt(gsx[...], wp[...]).astype(BF)
    e_lane = lax.rem(iota((8, T), 1), 4)
    upper = e_lane >= 2
    odd = lax.rem(e_lane, 2) == 1
    stay = (iota((8, T), 0) >= 4) == odd

    def some(j, carry):
        hots, sides = [], []
        for i in range(GP):
            g = j * GP + i
            row = idx[pl.ds(g, 1), :]
            hots.append(onehot(iota((256, T), 0) == jnp.bitwise_and(row, 255)))
            hi_of = jnp.right_shift(row, 8)
            lhs = jnp.concatenate(
                [
                    jnp.concatenate(
                        [
                            go[pl.ds(pl.multiple_of(g * 32 + 16 * q, 16), 16), 128 * ch : 128 * ch + 128]
                            for q in range(2)
                        ],
                        axis=1,
                    )
                    for ch in range(16)
                ],
                axis=0,
            )
            at = pl.multiple_of(g * T, T)
            zero = jnp.zeros((128, 128), BF)
            side = jnp.concatenate(
                [
                    jnp.concatenate([bas[pl.ds(at, 128), :], zero], axis=1),
                    jnp.concatenate([zero, bas[pl.ds(at + 128, 128), :]], axis=1),
                ],
                axis=0,
            )
            full = dot_nt(lhs, side)
            picked = [
                jnp.where(upper, full[16 * ch + 8 : 16 * ch + 16], full[16 * ch : 16 * ch + 8])
                for ch in range(16)
            ]
            grads = []
            for v in range(8):
                z0, z1 = picked[2 * v], picked[2 * v + 1]
                here = jnp.where(odd, z1, z0)
                there = jnp.where(odd, z0, z1)
                grads.append(jnp.where(stay, here, pltpu.roll(there, 4, 0)))
            grad = jnp.concatenate(grads, axis=0).astype(BF)
            sides.append(
                jnp.concatenate([grad * onehot(hi_of == hi) for hi in range(8)], axis=0)
            )
        acc[...] += dot_nt(jnp.concatenate(sides, axis=1), jnp.concatenate(hots, axis=1))
        return carry

    lax.fori_loop(0, GS // GP, some, 0)

    @pl.when(step == pl.num_programs(0) - 1)
    def _():
        def back(o):
            return remote(ret_send.at[o], ret_recv.at[o], r_send.at[o], r_recv.at[o], graph_at(-shifts[o]))

        for o in range(NL):
            part = acc[64 * (4 + o) : 64 * (4 + o) + 64, :]
            ret_send[o] = jnp.concatenate([part[:, :128], part[:, 128:]], axis=0).T.astype(BF)
            back(o).start()
        for i in range(4):
            m = pl.ds(256 * i, 256)
            pre_edge = dot(msg[m, :], w_edge[...])
            s_edge[m, :] = slope(pre_edge)
            hidden = silu(pre_edge).astype(BF)
            hid[m, :] = hidden
            s_down[m, :] = slope(dot_nt(hidden, w_down[...]))
        hots, backs = [], []
        for o in range(NL):
            picks = jnp.where(iota((1, CAP), 1) < count[0, o], rows[o : o + 1, :], -1)
            hots.append(onehot(iota((E, CAP), 0) == picks))
        for o in range(NL):
            back(o).wait()
            backs.append(unfold(ret_recv[o]))
        far = dot(jnp.concatenate(hots, axis=1), jnp.concatenate(backs, axis=0))
        downs = jnp.zeros((D, TW), F32)
        for i in range(4):
            m = pl.ds(256 * i, 256)
            part = acc[64 * i : 64 * i + 64, :]
            own = jnp.concatenate([part[:, :128], part[:, 128:]], axis=0).T
            grad_down = ((far[256 * i : 256 * i + 256] + unfold(own)) * s_down[m, :]).astype(BF)
            downs = downs + dot_tn(hid[m, :], grad_down)
            gedge[m, :] = (dot(grad_down, w_down[...]) * s_edge[m, :]).astype(BF)
        edges = dot_tn(msg[...], gedge[...])
        both = jnp.concatenate(
            [edges * factor, downs * factor, jnp.zeros((D, TW), F32)], axis=1
        ).astype(BF)
        for i in range(n):
            late[i % 2, i // 2] = both[16 * i : 16 * i + 16]
        sibling = (dp, me + 1 - 2 * core)
        first = remote(late.at[1 - core], pair_in, p_send, p_recv, sibling)
        first.start()
        for i in range(4):
            m = pl.ds(256 * i, 256)
            grad_msg[m, :] = dot_nt(gedge[m, :], w_edge[...]).astype(BF)
        first.wait()
        pair_out[...] = (late[core].astype(F32) + pair_in[...].astype(F32)).astype(BF)

        def begin(d, carry):
            late_copy(d).start()
            return carry

        lax.fori_loop(1, chips, begin, 0)
        for c in swap(0, dp_e):
            c.wait()
        sum_e[...] = total(dp_e)

        def take(d, total_):
            late_copy(d).wait()
            return total_ + in_l[d].astype(F32)

        dp_l[0] = lax.fori_loop(1, chips, take, pair_out[chip].astype(F32)).astype(BF)
        for c in swap(1, dp_l):
            c.start()
        for c in swap(1, dp_l):
            c.wait()
        sum_l[...] = total(dp_l)


def bwd(factor, gsx, bas, idx, w_bil, early, msg, w_edge, w_down, rows, count):
    whole = lambda shape: pl.BlockSpec(shape, lambda i: (0,) * len(shape))
    n = lax.axis_size("graph")
    n_dp = lax.axis_size("dp")
    dma = pltpu.SemaphoreType.DMA
    return pl.pallas_call(
        functools.partial(bwd_kernel, factor, n, n_dp),
        grid=(STEPS,),
        out_shape=[
            jax.ShapeDtypeStruct((E, D), BF),
            jax.ShapeDtypeStruct((16, 1152), F32),
            jax.ShapeDtypeStruct((16, 640), F32),
        ],
        in_specs=[
            pl.BlockSpec((32 * GS, 256), lambda i: (i, 0)),
            pl.BlockSpec((T * GS, 128), lambda i: (i, 0)),
            pl.BlockSpec((GS, T), lambda i: (i, 0)),
            whole((B, 4096)), whole((n, 16, 1152)),
            whole((E, D)), whole((D, D)), whole((TW, D)), whole((NL, CAP)),
            pl.BlockSpec(memory_space=pltpu.SMEM),
        ],
        out_specs=[whole((E, D)), whole((16, 1152)), whole((16, 640))],
        scratch_shapes=[
            pltpu.VMEM((2048, 256), BF),
            pltpu.VMEM((32 * GS, 2048), BF),
            pltpu.VMEM((512, 256), F32),
            pltpu.VMEM((NL, 128, 128), BF),
            pltpu.VMEM((NL, 128, 128), BF),
            pltpu.VMEM((E, D), F32),
            pltpu.VMEM((E, D), BF),
            pltpu.VMEM((E, TW), F32),
            pltpu.VMEM((E, D), BF),
            pltpu.VMEM((2, n // 2, 16, 640), BF),
            pltpu.VMEM((n, 16, 1152), BF),
            pltpu.VMEM((n // 2, 16, 640), BF),
            pltpu.VMEM((n // 2, 16, 640), BF),
            pltpu.VMEM((n // 2, 16, 640), BF),
            pltpu.VMEM((n_dp, 16, 1152), BF),
            pltpu.VMEM((n_dp, 16, 640), BF),
            dma((n,)), dma((n,)), dma((n // 2,)), dma((n // 2,)), dma((NL,)), dma((NL,)),
            dma, dma, dma((2, n_dp)), dma((2, n_dp)),
        ],
        compiler_params=pltpu.CompilerParams(
            collective_id=1, has_side_effects=True, vmem_limit_bytes=VMEM_LIMIT
        ),
        name="triplets_back",
    )(gsx, bas, idx, w_bil, early, msg, w_edge, w_down, rows, count)


def last_kernel(grad_msg, e, l, o_msg, o_edge, o_down, o_bil, o_up):
    o_msg[...] = grad_msg[...]

    @pl.when(pl.program_id(0) == 0)
    def _():
        o_edge[...] = l[:, :D]
        o_down[...] = l[:, D : D + TW]
        square = jnp.concatenate([e[:, 128 * j : 128 * j + 128] for j in range(8)], axis=0).T
        o_bil[...] = square[:B]
        o_up[0] = e[:, 1024:1088]
        o_up[1] = e[:, 1088:1152]


def last(grad_msg, e, l):
    whole = lambda shape: pl.BlockSpec(shape, lambda i: (0,) * len(shape))
    rows = pl.BlockSpec((256, D), lambda i: (i, 0))
    return pl.pallas_call(
        last_kernel,
        grid=(4,),
        out_shape=[
            jax.ShapeDtypeStruct((E, D), BF),
            jax.ShapeDtypeStruct((16, D), F32),
            jax.ShapeDtypeStruct((16, TW), F32),
            jax.ShapeDtypeStruct((B, 128), F32),
            jax.ShapeDtypeStruct((2, 16, TW), F32),
        ],
        in_specs=[rows, whole((16, 1152)), whole((16, 640))],
        out_specs=[rows, whole((16, D)), whole((16, TW)), whole((B, 128)), whole((2, 16, TW))],
        name="outputs",
    )(grad_msg, e, l)


def body(
    messages, cotangent, triplet_basis, w_edge, w_down, w_bil, w_up,
    trip_src, send_rows, send_count, rev_src, edge_count,
):
    msg, cot = messages[0], cotangent[0]
    narrow = w_down.T
    rows = send_rows[0]
    factor = 1.0 / math.sqrt(lax.axis_size("dp") * lax.axis_size("graph") * E)
    idx = trip_src[0].reshape(E // G, 2, 4, K).transpose(0, 1, 3, 2).reshape(E // G, T)
    outer, bas, state, far = fwd(
        msg, cot, w_edge, narrow, rows, send_count, triplet_basis[0], idx, w_bil
    )
    gsx, early = mid(
        factor, state, outer, cot, far.reshape(NL * CAP, D), rev_src.reshape(8, 128), w_up, edge_count
    )
    grad_msg, e, l = bwd(factor, gsx, bas, idx, w_bil, early, msg, w_edge, narrow, rows, send_count)
    grad_msg, g_edge, g_down, g_bil, g_up = last(grad_msg, e, l)
    return grad_msg[None], g_edge, g_down, g_bil, g_up.transpose(0, 2, 1)


def solution(mesh):
    row = P("dp", "graph", None)
    flat = P("dp", "graph")
    return jax.shard_map(
        body,
        mesh=mesh,
        in_specs=(row, row, row, P(), P(), P(), P(), row, row, flat, flat, flat),
        out_specs=(
            row,
            P("graph", None),
            P("graph", None),
            P(None, "graph"),
            P(None, None, "graph"),
        ),
        check_vma=False,
    )
```

```python
import functools
import math

import jax
import jax.numpy as jnp
from jax import lax
from jax.experimental import pallas as pl
from jax.experimental.pallas import tpu as pltpu
from jax.sharding import PartitionSpec as P

INV_ROOT = 0.7071067811865476
BF = jnp.bfloat16
F32 = jnp.float32
MESH = pl.DeviceIdType.MESH
VMEM_LIMIT = 56 * 1024 * 1024

E = 1024
K = 32
B = 112
TW = 64
D = 512
CAP = 256
NL = 4
G = 8
T = G * K


def offsets(count):
    return [(which // 2 + 1) * (1 - 2 * (which % 2)) for which in range(count)]


def sigmoid(v):
    return 0.5 + 0.5 * jnp.tanh(0.5 * v)


def silu(v):
    return v * sigmoid(v)


def slope(v):
    s = sigmoid(v)
    return s * (1.0 + v * (1.0 - s))


def iota(shape, dim):
    return lax.broadcasted_iota(jnp.int32, shape, dim)


def dot(a, b):
    return jnp.dot(a, b, preferred_element_type=F32)


def dot_nt(a, b):
    return lax.dot_general(a, b, (((1,), (1,)), ((), ())), preferred_element_type=F32)


def dot_tn(a, b):
    return lax.dot_general(a, b, (((0,), (0,)), ((), ())), preferred_element_type=F32)


def onehot(cond):
    return jnp.where(cond, 1.0, 0.0).astype(BF)


GS = 16
GP = 4
STEPS = E // (G * GS)


def graph_at(distance):
    n = lax.axis_size("graph")
    return (lax.axis_index("dp"), lax.rem(lax.axis_index("graph") + (distance + n), n))


def remote(src, dst, send, recv, where):
    return pltpu.make_async_remote_copy(
        src, dst, send, recv, device_id=where, device_id_type=MESH
    )


def greet(where):
    pl.semaphore_signal(
        pltpu.get_barrier_semaphore(), inc=1, device_id=where, device_id_type=MESH
    )


BE = 128
MIDDLE = STEPS
BACK = STEPS + E // BE
ALL = BACK + STEPS
SWAP = BACK + 5


def load_w(wp, w_bil):
    wp[...] = jnp.zeros_like(wp)
    for ch in range(16):
        wp[128 * ch : 128 * ch + B, :] = w_bil[:, 256 * ch : 256 * ch + 256]


def fold(rows):
    half = rows.shape[0] // 2
    return jnp.concatenate([rows[:half], rows[half:]], axis=1)


def unfold(rows):
    return jnp.concatenate([rows[:, :TW], rows[:, TW:]], axis=0)


def kernel(factor, n, n_dp, msg, cot, w_edge, w_down, w_up, rows, rev, count, live, basis, idx, w_bil,
           grad_msg, sum_e, sum_l,
           red, pool_t, wp, sbuf, outer, bas, state, red_send, red_recv, cot_send, cot_recv,
           gsx, bil, up, early, go, acc, ret_send, ret_recv, s_edge, hid, s_down, gedge,
           late, in_e, pair_in, pair_out, in_l, dp_e, dp_l,
           send, recv, e_send, e_recv, l_send, l_recv, r_send, r_recv, p_send, p_recv, d_send, d_recv):
    step = pl.program_id(0)
    shifts = offsets(NL)
    me = lax.axis_index("graph")
    dp = lax.axis_index("dp")
    core = lax.rem(me, 2)
    chip = me // 2
    chips = n // 2

    def red_copy(o):
        where = graph_at(shifts[o])
        return remote(red_send.at[o], red_recv.at[o], send.at[0, o], recv.at[0, o], where)

    def cot_copy(o):
        where = graph_at(shifts[o])
        return remote(cot_send.at[o], cot_recv.at[o], send.at[1, o], recv.at[1, o], where)

    def early_copy(d):
        to = lax.rem(me + d, n)
        return remote(early.at[to], in_e.at[d], e_send.at[d], e_recv.at[d], (dp, to))

    def late_copy(d):
        to = lax.rem(chip + d, chips)
        return remote(pair_out.at[to], in_l.at[d], l_send.at[d], l_recv.at[d], (dp, 2 * to + core))

    def swap(which, buf):
        out = []
        for d in range(1, n_dp):
            where = (lax.rem(dp + d, n_dp), me)
            out.append(remote(buf.at[0], buf.at[d], d_send.at[which, d], d_recv.at[which, d], where))
        return out

    def total(buf):
        terms = [buf[d].astype(F32) for d in range(n_dp)]
        out = jnp.zeros_like(terms[0])
        for source in range(n_dp):
            for d in range(n_dp):
                hit = lax.rem(dp + (n_dp - d), n_dp) == source
                out = out + jnp.where(hit, terms[d], 0.0)
        return out

    @pl.when(step == 0)
    def _():
        def hello(d, carry):
            greet((dp, lax.rem(me + d, n)))
            return carry

        lax.fori_loop(1, n, hello, 0)
        for d in range(1, n_dp):
            greet((lax.rem(dp + d, n_dp), me))
        for i in range(4):
            m = pl.ds(256 * i, 256)
            hidden = silu(dot(msg[m, :], w_edge[...])).astype(BF)
            red[m, :] = silu(dot_nt(hidden, w_down[...])).astype(BF)
        lane = iota((1, CAP), 1)
        lists = []
        for o in range(NL):
            lists.append(jnp.where(lane < count[0, o], rows[o : o + 1, :], -1))
        picks = jnp.concatenate(lists + lists, axis=0).T
        wide = iota((CAP, E), 1)
        for o in range(NL):
            red_send[o] = fold(dot(onehot(wide == picks[:, o : o + 1]), red[...]).astype(BF))
        pl.semaphore_wait(pltpu.get_barrier_semaphore(), n - 1 + n_dp - 1)
        for o in range(NL):
            red_copy(o).start()
        for o in range(NL):
            cot_send[o] = dot(onehot(wide == picks[:, o : o + 1]), cot[...]).astype(BF)
            cot_copy(o).start()
        load_w(wp, w_bil)
        for hi in range(8):
            if hi < 4:
                src = fold(red[256 * hi : 256 * hi + 256, :])
            else:
                red_copy(hi - 4).wait_recv()
                src = red_recv[hi - 4]
            flip = src.astype(F32).T
            pool_t[64 * hi : 64 * hi + 64, :] = jnp.concatenate(
                [flip[:64], flip[64:]], axis=1
            ).astype(BF)

        bil[...] = jnp.zeros_like(bil)
        up[...] = jnp.zeros_like(up)
        acc[...] = jnp.zeros_like(acc)

    @pl.when(step < MIDDLE)
    def _():
        part = step
        keep = onehot(lax.rem(iota((16, T), 1), 4) == iota((16, T), 0) // 4)
        low = iota((8, T), 0) < 4
        low1 = iota((8, 128), 0) < 4

        def some(j, carry):
            hots, his = [], []
            for i in range(GP):
                row = idx[pl.ds(part * GS + j * GP + i, 1), :]
                hots.append(onehot(iota((256, T), 0) == jnp.bitwise_and(row, 255)))
                his.append(jnp.right_shift(row, 8))
            found = dot(pool_t[...], jnp.concatenate(hots, axis=1)).astype(BF)
            founds = [found[:, T * i : T * i + T] for i in range(GP)]
            for i in range(GP):
                g = j * GP + i
                wide = basis[pl.ds(pl.multiple_of(g * G, G), G), :].astype(F32)
                pieces = []
                for k in range(K):
                    piece = wide[:, k * B : (k + 1) * B]
                    pieces.append(jnp.concatenate([piece, jnp.zeros((G, 128 - B), F32)], axis=1))
                first, second = [], []
                for k in range(0, K, 2):
                    x, y = pieces[k], pieces[k + 1]
                    z = pltpu.roll(jnp.where(low1, y, x), 4, 0)
                    first.append(jnp.where(low1, x, z))
                    second.append(jnp.where(low1, z, y))
                first = jnp.concatenate(first, axis=0).astype(BF)
                second = jnp.concatenate(second, axis=0).astype(BF)
                zero = jnp.zeros((128, 128), BF)
                at = pl.multiple_of((part * GS + g) * T, T)
                bas[pl.ds(at, 128), :] = first
                bas[pl.ds(at + 128, 128), :] = second
                rhs = jnp.concatenate(
                    [jnp.concatenate([first, zero], axis=1), jnp.concatenate([zero, second], axis=1)], axis=0
                )
                got = founds[i][:64] * onehot(his[i] == 0)
                for hi in range(1, 8):
                    got = got + founds[i][64 * hi : 64 * hi + 64] * onehot(his[i] == hi)
                got = got.astype(F32)
                tiles = []
                for v in range(8):
                    x = got[8 * v : 8 * v + 8]
                    y = pltpu.roll(x, 4, 0)
                    for d in (jnp.where(low, x, y), jnp.where(low, y, x)):
                        tiles.append(jnp.concatenate([d, d], axis=0).astype(BF) * keep)
                lhs = jnp.concatenate(tiles, axis=0)
                out = dot(lhs, rhs).astype(BF)
                for q in range(2):
                    for ch in range(16):
                        outer[pl.ds(pl.multiple_of((part * GS + g) * 32 + 16 * q, 16), 16), 128 * ch : 128 * ch + 128] = (
                            out[16 * ch : 16 * ch + 16, 128 * q : 128 * q + 128]
                        )
            return carry

        lax.fori_loop(0, GS // GP, some, 0)
        tall = 32 * GS
        full = dot(outer[pl.ds(pl.multiple_of(part * tall, tall), tall), :], wp[...])
        full = jnp.where(lax.rem(iota((tall, 256), 0), 4) == iota((tall, 256), 1) // 64, full, 0.0)
        full = full + pltpu.roll(full, 1, 0)
        full = full + pltpu.roll(full, 2, 0)
        sbuf[...] = full[:, :128] + full[:, 128:]
        picked = sbuf[pl.ds(3, G * GS, stride=4), :]
        state[pl.ds(pl.multiple_of(part * (G * GS), G * GS), G * GS), :] = (picked + pltpu.roll(picked, 64, 1)).astype(BF)

    @pl.when(step == MIDDLE)
    def _():
        for o in range(NL):
            red_copy(o).wait_send()
            cot_copy(o).wait()

    @pl.when((step >= MIDDLE) & (step < BACK))
    def _():
        part = step - MIDDLE
        at = pl.multiple_of(part * BE, BE)
        tall = pl.multiple_of(part * (4 * BE), 4 * BE)
        st = state[pl.ds(at, BE), :][:, :TW]
        alive = iota((BE, D), 0) + at < live[0, 0]
        scaled = jnp.where(alive, cot[pl.ds(at, BE), :].astype(F32) * INV_ROOT, 0.0)
        grad_ca = (scaled * slope(dot(st, w_up[0]))).astype(BF)
        row = rev[pl.ds(part, 1), :]
        col = jnp.concatenate([row] * 8, axis=0).T[:, :1]
        mirror = dot(onehot(iota((BE, E), 1) == col), cot[...])
        mirror = mirror + dot(onehot(iota((BE, NL * CAP), 1) + E == col), cot_recv[...].reshape(NL * CAP, D))
        grad_ac = (mirror * INV_ROOT * slope(dot(st, w_up[1]))).astype(BF)
        up[:TW, :] += dot_tn(st, grad_ca)
        up[TW:, :] += dot_tn(st, grad_ac)
        own = dot_nt(grad_ca, jnp.concatenate([w_up[0]] * 4, axis=0))
        back = dot_nt(grad_ac, jnp.concatenate([w_up[1]] * 4, axis=0)).astype(BF)
        grad_state = (own + back.astype(F32)).astype(BF)
        spread = onehot(iota((4 * BE, BE), 0) // 4 == iota((4 * BE, BE), 1))
        big = dot(spread, grad_state)
        big = jnp.where(lax.rem(iota((4 * BE, 256), 0), 4) == iota((4 * BE, 256), 1) // 64, big, 0.0)
        big = big.astype(BF)
        gsx[pl.ds(tall, 4 * BE), :] = big
        bil[...] += dot_tn(big, outer[pl.ds(tall, 4 * BE), :])

    @pl.when(step == BACK - 1)
    def _():
        turned = (up[...] * factor).T.astype(BF)
        for i in range(32):
            early[i, :, 1024:1152] = turned[16 * i : 16 * i + 16]
            r, c = (i % 2) * 128, (i // 2) * 128
            for j in range(8):
                early[i, :, 128 * j : 128 * j + 128] = (
                    bil[r + 16 * j : r + 16 * j + 16, c : c + 128] * factor
                ).astype(BF)

        def begin(d, carry):
            early_copy(d).start()
            return carry

        lax.fori_loop(1, n, begin, 0)

    @pl.when(step == SWAP)
    def _():
        def take(d, total_):
            early_copy(d).wait()
            return total_ + in_e[d].astype(F32)

        dp_e[0] = lax.fori_loop(1, n, take, early[me].astype(F32)).astype(BF)
        for c in swap(0, dp_e):
            c.start()

    @pl.when(step >= BACK)
    def _():
        part = step - BACK
        go[...] = dot_nt(gsx[pl.ds(pl.multiple_of(part * (32 * GS), 32 * GS), 32 * GS), :], wp[...]).astype(BF)
        e_lane = lax.rem(iota((8, T), 1), 4)
        upper = e_lane >= 2
        odd = lax.rem(e_lane, 2) == 1
        stay = (iota((8, T), 0) >= 4) == odd

        def some(j, carry):
            hots, sides = [], []
            for i in range(GP):
                g = j * GP + i
                row = idx[pl.ds(part * GS + g, 1), :]
                hots.append(onehot(iota((256, T), 0) == jnp.bitwise_and(row, 255)))
                hi_of = jnp.right_shift(row, 8)
                lhs = jnp.concatenate(
                    [
                        jnp.concatenate(
                            [
                                go[pl.ds(pl.multiple_of(g * 32 + 16 * q, 16), 16), 128 * ch : 128 * ch + 128]
                                for q in range(2)
                            ],
                            axis=1,
                        )
                        for ch in range(16)
                    ],
                    axis=0,
                )
                at = pl.multiple_of((part * GS + g) * T, T)
                zero = jnp.zeros((128, 128), BF)
                side = jnp.concatenate(
                    [
                        jnp.concatenate([bas[pl.ds(at, 128), :], zero], axis=1),
                        jnp.concatenate([zero, bas[pl.ds(at + 128, 128), :]], axis=1),
                    ],
                    axis=0,
                )
                full = dot_nt(lhs, side)
                picked = [
                    jnp.where(upper, full[16 * ch + 8 : 16 * ch + 16], full[16 * ch : 16 * ch + 8])
                    for ch in range(16)
                ]
                grads = []
                for v in range(8):
                    z0, z1 = picked[2 * v], picked[2 * v + 1]
                    here = jnp.where(odd, z1, z0)
                    there = jnp.where(odd, z0, z1)
                    grads.append(jnp.where(stay, here, pltpu.roll(there, 4, 0)))
                grad = jnp.concatenate(grads, axis=0).astype(BF)
                sides.append(
                    jnp.concatenate([grad * onehot(hi_of == hi) for hi in range(8)], axis=0)
                )
            acc[...] += dot_nt(jnp.concatenate(sides, axis=1), jnp.concatenate(hots, axis=1))
            return carry

        lax.fori_loop(0, GS // GP, some, 0)

    @pl.when(step == ALL - 1)
    def _():
        def back(o):
            return remote(ret_send.at[o], ret_recv.at[o], r_send.at[o], r_recv.at[o], graph_at(-shifts[o]))

        for o in range(NL):
            part = acc[64 * (4 + o) : 64 * (4 + o) + 64, :]
            ret_send[o] = jnp.concatenate([part[:, :128], part[:, 128:]], axis=0).T.astype(BF)
            back(o).start()
        for i in range(4):
            m = pl.ds(256 * i, 256)
            pre_edge = dot(msg[m, :], w_edge[...])
            s_edge[m, :] = slope(pre_edge)
            hidden = silu(pre_edge).astype(BF)
            hid[m, :] = hidden
            s_down[m, :] = slope(dot_nt(hidden, w_down[...]))
        hots, backs = [], []
        for o in range(NL):
            picks = jnp.where(iota((1, CAP), 1) < count[0, o], rows[o : o + 1, :], -1)
            hots.append(onehot(iota((E, CAP), 0) == picks))
        for o in range(NL):
            back(o).wait()
            backs.append(unfold(ret_recv[o]))
        far = dot(jnp.concatenate(hots, axis=1), jnp.concatenate(backs, axis=0))
        downs = jnp.zeros((D, TW), F32)
        for i in range(4):
            m = pl.ds(256 * i, 256)
            part = acc[64 * i : 64 * i + 64, :]
            own = jnp.concatenate([part[:, :128], part[:, 128:]], axis=0).T
            grad_down = ((far[256 * i : 256 * i + 256] + unfold(own)) * s_down[m, :]).astype(BF)
            downs = downs + dot_tn(hid[m, :], grad_down)
            gedge[m, :] = (dot(grad_down, w_down[...]) * s_edge[m, :]).astype(BF)
        edges = dot_tn(msg[...], gedge[...])
        both = jnp.concatenate(
            [edges * factor, downs * factor, jnp.zeros((D, TW), F32)], axis=1
        ).astype(BF)
        for i in range(n):
            late[i % 2, i // 2] = both[16 * i : 16 * i + 16]
        sibling = (dp, me + 1 - 2 * core)
        first = remote(late.at[1 - core], pair_in, p_send, p_recv, sibling)
        first.start()
        for i in range(4):
            m = pl.ds(256 * i, 256)
            grad_msg[m, :] = dot_nt(gedge[m, :], w_edge[...]).astype(BF)
        first.wait()
        pair_out[...] = (late[core].astype(F32) + pair_in[...].astype(F32)).astype(BF)

        def begin(d, carry):
            late_copy(d).start()
            return carry

        lax.fori_loop(1, chips, begin, 0)
        for c in swap(0, dp_e):
            c.wait()
        sum_e[...] = total(dp_e)

        def take(d, total_):
            late_copy(d).wait()
            return total_ + in_l[d].astype(F32)

        dp_l[0] = lax.fori_loop(1, chips, take, pair_out[chip].astype(F32)).astype(BF)
        for c in swap(1, dp_l):
            c.start()
        for c in swap(1, dp_l):
            c.wait()
        sum_l[...] = total(dp_l)


def run(factor, msg, cot, w_edge, w_down, w_up, rows, rev, count, live, basis, idx, w_bil):
    whole = lambda shape: pl.BlockSpec(
        shape, lambda i: (0,) * len(shape), pipeline_mode=pl.Buffered(1)
    )
    smem = pl.BlockSpec(memory_space=pltpu.SMEM)
    n = lax.axis_size("graph")
    n_dp = lax.axis_size("dp")
    dma = pltpu.SemaphoreType.DMA
    bf = lambda *shape: pltpu.VMEM(shape, BF)
    f32 = lambda *shape: pltpu.VMEM(shape, F32)
    return pl.pallas_call(
        functools.partial(kernel, factor, n, n_dp),
        grid=(ALL,),
        out_shape=[
            jax.ShapeDtypeStruct((E, D), BF),
            jax.ShapeDtypeStruct((16, 1152), F32),
            jax.ShapeDtypeStruct((16, 640), F32),
        ],
        in_specs=[
            whole((E, D)), whole((E, D)), whole((D, D)), whole((TW, D)), whole((2, TW, D)),
            whole((NL, CAP)), whole((8, 128)), smem, smem,
            pl.BlockSpec((G * GS, K * B), lambda i: (jnp.minimum(i, STEPS - 1), 0)),
            whole((E // G, T)), whole((B, 4096)),
        ],
        out_specs=[whole((E, D)), whole((16, 1152)), whole((16, 640))],
        scratch_shapes=[
            bf(E, TW), bf(512, 256), bf(2048, 256), f32(32 * GS, 128),
            bf(4 * E, 2048), bf(E * K, 128), bf(E, 128),
            bf(NL, 128, 128), bf(NL, 128, 128), bf(NL, CAP, D), bf(NL, CAP, D),
            bf(4 * E, 256), f32(256, 2048), f32(2 * TW, D), bf(n, 16, 1152),
            bf(32 * GS, 2048), f32(512, 256), bf(NL, 128, 128), bf(NL, 128, 128),
            f32(E, D), bf(E, D), f32(E, TW), bf(E, D),
            bf(2, n // 2, 16, 640), bf(n, 16, 1152),
            bf(n // 2, 16, 640), bf(n // 2, 16, 640), bf(n // 2, 16, 640),
            bf(n_dp, 16, 1152), bf(n_dp, 16, 640),
            dma((2, NL)), dma((2, NL)), dma((n,)), dma((n,)), dma((n // 2,)), dma((n // 2,)),
            dma((NL,)), dma((NL,)), dma, dma, dma((2, n_dp)), dma((2, n_dp)),
        ],
        compiler_params=pltpu.CompilerParams(
            collective_id=0, has_side_effects=True, vmem_limit_bytes=VMEM_LIMIT
        ),
        name="triplets",
    )(msg, cot, w_edge, w_down, w_up, rows, rev, count, live, basis, idx, w_bil)


def last_kernel(grad_msg, e, l, o_msg, o_edge, o_down, o_bil, o_up):
    o_msg[...] = grad_msg[...]

    @pl.when(pl.program_id(0) == 0)
    def _():
        o_edge[...] = l[:, :D]
        o_down[...] = l[:, D : D + TW]
        square = jnp.concatenate([e[:, 128 * j : 128 * j + 128] for j in range(8)], axis=0).T
        o_bil[...] = square[:B]
        o_up[0] = e[:, 1024:1088]
        o_up[1] = e[:, 1088:1152]


def last(grad_msg, e, l):
    whole = lambda shape: pl.BlockSpec(shape, lambda i: (0,) * len(shape))
    rows = pl.BlockSpec((256, D), lambda i: (i, 0))
    return pl.pallas_call(
        last_kernel,
        grid=(4,),
        out_shape=[
            jax.ShapeDtypeStruct((E, D), BF),
            jax.ShapeDtypeStruct((16, D), F32),
            jax.ShapeDtypeStruct((16, TW), F32),
            jax.ShapeDtypeStruct((B, 128), F32),
            jax.ShapeDtypeStruct((2, 16, TW), F32),
        ],
        in_specs=[rows, whole((16, 1152)), whole((16, 640))],
        out_specs=[rows, whole((16, D)), whole((16, TW)), whole((B, 128)), whole((2, 16, TW))],
        name="outputs",
    )(grad_msg, e, l)


def body(
    messages, cotangent, triplet_basis, w_edge, w_down, w_bil, w_up,
    trip_src, send_rows, send_count, rev_src, edge_count,
):
    factor = 1.0 / math.sqrt(lax.axis_size("dp") * lax.axis_size("graph") * E)
    idx = trip_src[0].reshape(E // G, 2, 4, K).transpose(0, 1, 3, 2).reshape(E // G, T)
    grad_msg, e, l = run(
        factor, messages[0], cotangent[0], w_edge, w_down.T, w_up, send_rows[0],
        rev_src.reshape(8, 128), send_count, edge_count, triplet_basis[0], idx, w_bil,
    )
    grad_msg, g_edge, g_down, g_bil, g_up = last(grad_msg, e, l)
    return grad_msg[None], g_edge, g_down, g_bil, g_up.transpose(0, 2, 1)


def solution(mesh):
    row = P("dp", "graph", None)
    flat = P("dp", "graph")
    return jax.shard_map(
        body,
        mesh=mesh,
        in_specs=(row, row, row, P(), P(), P(), P(), row, row, flat, flat, flat),
        out_specs=(
            row,
            P("graph", None),
            P("graph", None),
            P(None, "graph"),
            P(None, None, "graph"),
        ),
        check_vma=False,
    )
```

```python
import functools
import math

import jax
import jax.numpy as jnp
from jax import lax
from jax.experimental import pallas as pl
from jax.experimental.pallas import tpu as pltpu
from jax.sharding import PartitionSpec as P

INV_ROOT = 0.7071067811865476
BF = jnp.bfloat16
F32 = jnp.float32
MESH = pl.DeviceIdType.MESH
VMEM_LIMIT = 56 * 1024 * 1024

E = 1024
K = 32
B = 112
TW = 64
D = 512
CAP = 256
NL = 4
G = 8
T = G * K


def offsets(count):
    return [(which // 2 + 1) * (1 - 2 * (which % 2)) for which in range(count)]


def sigmoid(v):
    return 0.5 + 0.5 * jnp.tanh(0.5 * v)


def silu(v):
    return v * sigmoid(v)


def slope(v):
    s = sigmoid(v)
    return s * (1.0 + v * (1.0 - s))


def iota(shape, dim):
    return lax.broadcasted_iota(jnp.int32, shape, dim)


def dot(a, b):
    return jnp.dot(a, b, preferred_element_type=F32)


def dot_nt(a, b):
    return lax.dot_general(a, b, (((1,), (1,)), ((), ())), preferred_element_type=F32)


def dot_tn(a, b):
    return lax.dot_general(a, b, (((0,), (0,)), ((), ())), preferred_element_type=F32)


def onehot(cond):
    return jnp.where(cond, 1.0, 0.0).astype(BF)


GS = 16
GP = 8
BP = 16
STEPS = E // (G * GS)


def graph_at(distance):
    n = lax.axis_size("graph")
    return (lax.axis_index("dp"), lax.rem(lax.axis_index("graph") + (distance + n), n))


def remote(src, dst, send, recv, where):
    return pltpu.make_async_remote_copy(
        src, dst, send, recv, device_id=where, device_id_type=MESH
    )


def greet(where):
    pl.semaphore_signal(
        pltpu.get_barrier_semaphore(), inc=1, device_id=where, device_id_type=MESH
    )


BE = 256
MIDDLE = STEPS
BACK = STEPS + E // BE
ALL = BACK + STEPS
SWAP = BACK + 5


def load_w(wp, w_bil):
    wp[...] = jnp.zeros_like(wp)
    for ch in range(16):
        wp[128 * ch : 128 * ch + B, :] = w_bil[:, 256 * ch : 256 * ch + 256]


def fold(rows):
    half = rows.shape[0] // 2
    return jnp.concatenate([rows[:half], rows[half:]], axis=1)


def unfold(rows):
    return jnp.concatenate([rows[:, :TW], rows[:, TW:]], axis=0)


def kernel(factor, n, n_dp, msg, cot, w_edge, w_down, w_up, rows, rev, count, live, basis, idx, w_bil,
           grad_msg, sum_e, sum_l,
           red, pool_t, wp, sbuf, outer, bas, state, red_send, red_recv, cot_send, cot_recv,
           gsx, bil, up, early, go, acc, ret_send, ret_recv, s_edge, hid, s_down, gedge,
           late, in_e, pair_in, pair_out, in_l, dp_e, dp_l,
           send, recv, e_send, e_recv, l_send, l_recv, r_send, r_recv, p_send, p_recv, d_send, d_recv):
    step = pl.program_id(0)
    shifts = offsets(NL)
    me = lax.axis_index("graph")
    dp = lax.axis_index("dp")
    core = lax.rem(me, 2)
    chip = me // 2
    chips = n // 2

    def red_copy(o):
        where = graph_at(shifts[o])
        return remote(red_send.at[o], red_recv.at[o], send.at[0, o], recv.at[0, o], where)

    def cot_copy(o):
        where = graph_at(shifts[o])
        return remote(cot_send.at[o], cot_recv.at[o], send.at[1, o], recv.at[1, o], where)

    def early_copy(d):
        to = lax.rem(me + d, n)
        return remote(early.at[to], in_e.at[d], e_send.at[d], e_recv.at[d], (dp, to))

    def late_copy(to, d):
        return remote(pair_out.at[to], in_l.at[d], l_send.at[d], l_recv.at[d], (dp, 2 * to + core))

    def swap(which, buf):
        out = []
        for d in range(1, n_dp):
            where = (lax.rem(dp + d, n_dp), me)
            out.append(remote(buf.at[0], buf.at[d], d_send.at[which, d], d_recv.at[which, d], where))
        return out

    def total(buf):
        terms = [buf[d].astype(F32) for d in range(n_dp)]
        out = jnp.zeros_like(terms[0])
        for source in range(n_dp):
            for d in range(n_dp):
                hit = lax.rem(dp + (n_dp - d), n_dp) == source
                out = out + jnp.where(hit, terms[d], 0.0)
        return out

    @pl.when(step == 0)
    def _():
        def hello(d, carry):
            greet((dp, lax.rem(me + d, n)))
            return carry

        lax.fori_loop(1, n, hello, 0)
        for d in range(1, n_dp):
            greet((lax.rem(dp + d, n_dp), me))
        for i in range(4):
            m = pl.ds(256 * i, 256)
            hidden = silu(dot(msg[m, :], w_edge[...])).astype(BF)
            red[m, :] = silu(dot_nt(hidden, w_down[...])).astype(BF)
        lane = iota((1, CAP), 1)
        lists = []
        for o in range(NL):
            lists.append(jnp.where(lane < count[0, o], rows[o : o + 1, :], -1))
        picks = jnp.concatenate(lists + lists, axis=0).T
        wide = iota((CAP, E), 1)
        for o in range(NL):
            red_send[o] = fold(dot(onehot(wide == picks[:, o : o + 1]), red[...]).astype(BF))
        pl.semaphore_wait(pltpu.get_barrier_semaphore(), n - 1 + n_dp - 1)
        for o in range(NL):
            red_copy(o).start()
        for o in range(NL):
            cot_send[o] = dot(onehot(wide == picks[:, o : o + 1]), cot[...]).astype(BF)
            cot_copy(o).start()
        load_w(wp, w_bil)
        for hi in range(8):
            if hi < 4:
                src = fold(red[256 * hi : 256 * hi + 256, :])
            else:
                red_copy(hi - 4).wait_recv()
                src = red_recv[hi - 4]
            flip = src.astype(F32).T
            pool_t[64 * hi : 64 * hi + 64, :] = jnp.concatenate(
                [flip[:64], flip[64:]], axis=1
            ).astype(BF)

        bil[...] = jnp.zeros_like(bil)
        up[...] = jnp.zeros_like(up)
        acc[...] = jnp.zeros_like(acc)

    @pl.when(step < MIDDLE)
    def _():
        part = step
        keep = onehot(lax.rem(iota((16, T), 1), 4) == iota((16, T), 0) // 4)
        low = iota((8, T), 0) < 4
        low1 = iota((8, 128), 0) < 4

        def some(j, carry):
            hots, his = [], []
            for i in range(GP):
                row = idx[pl.ds(part * GS + j * GP + i, 1), :]
                hots.append(onehot(iota((256, T), 0) == jnp.bitwise_and(row, 255)))
                his.append(jnp.right_shift(row, 8))
            found = dot(pool_t[...], jnp.concatenate(hots, axis=1)).astype(BF)
            founds = [found[:, T * i : T * i + T] for i in range(GP)]
            for i in range(GP):
                g = j * GP + i
                wide = basis[pl.ds(pl.multiple_of(g * G, G), G), :].astype(F32)
                pieces = []
                for k in range(K):
                    piece = wide[:, k * B : (k + 1) * B]
                    pieces.append(jnp.concatenate([piece, jnp.zeros((G, 128 - B), F32)], axis=1))
                first, second = [], []
                for k in range(0, K, 2):
                    x, y = pieces[k], pieces[k + 1]
                    z = pltpu.roll(jnp.where(low1, y, x), 4, 0)
                    first.append(jnp.where(low1, x, z))
                    second.append(jnp.where(low1, z, y))
                first = jnp.concatenate(first, axis=0).astype(BF)
                second = jnp.concatenate(second, axis=0).astype(BF)
                zero = jnp.zeros((128, 128), BF)
                at = pl.multiple_of((part * GS + g) * T, T)
                bas[pl.ds(at, 128), :] = first
                bas[pl.ds(at + 128, 128), :] = second
                rhs = jnp.concatenate(
                    [jnp.concatenate([first, zero], axis=1), jnp.concatenate([zero, second], axis=1)], axis=0
                )
                got = founds[i][:64] * onehot(his[i] == 0)
                for hi in range(1, 8):
                    got = got + founds[i][64 * hi : 64 * hi + 64] * onehot(his[i] == hi)
                got = got.astype(F32)
                tiles = []
                for v in range(8):
                    x = got[8 * v : 8 * v + 8]
                    y = pltpu.roll(x, 4, 0)
                    for d in (jnp.where(low, x, y), jnp.where(low, y, x)):
                        tiles.append(jnp.concatenate([d, d], axis=0).astype(BF) * keep)
                lhs = jnp.concatenate(tiles, axis=0)
                out = dot(lhs, rhs).astype(BF)
                for q in range(2):
                    for ch in range(16):
                        outer[pl.ds(pl.multiple_of((part * GS + g) * 32 + 16 * q, 16), 16), 128 * ch : 128 * ch + 128] = (
                            out[16 * ch : 16 * ch + 16, 128 * q : 128 * q + 128]
                        )
            return carry

        lax.fori_loop(0, GS // GP, some, 0)
        tall = 32 * GS
        full = dot(outer[pl.ds(pl.multiple_of(part * tall, tall), tall), :], wp[...])
        full = jnp.where(lax.rem(iota((tall, 256), 0), 4) == iota((tall, 256), 1) // 64, full, 0.0)
        full = full + pltpu.roll(full, 1, 0)
        full = full + pltpu.roll(full, 2, 0)
        sbuf[...] = full[:, :128] + full[:, 128:]
        picked = sbuf[pl.ds(3, G * GS, stride=4), :]
        state[pl.ds(pl.multiple_of(part * (G * GS), G * GS), G * GS), :] = (picked + pltpu.roll(picked, 64, 1)).astype(BF)

    @pl.when(step == MIDDLE)
    def _():
        for o in range(NL):
            red_copy(o).wait_send()
            cot_copy(o).wait()

    @pl.when((step >= MIDDLE) & (step < BACK))
    def _():
        part = step - MIDDLE
        at = pl.multiple_of(part * BE, BE)
        tall = pl.multiple_of(part * (4 * BE), 4 * BE)
        st = state[pl.ds(at, BE), :][:, :TW]
        alive = iota((BE, D), 0) + at < live[0, 0]
        scaled = jnp.where(alive, cot[pl.ds(at, BE), :].astype(F32) * INV_ROOT, 0.0)
        grad_ca = (scaled * slope(dot(st, w_up[0]))).astype(BF)
        col = jnp.concatenate(
            [
                jnp.concatenate([rev[pl.ds(part * (BE // 128) + h, 1), :]] * 8, axis=0).T[:, :1]
                for h in range(BE // 128)
            ],
            axis=0,
        )
        mirror = dot(onehot(iota((BE, E), 1) == col), cot[...])
        mirror = mirror + dot(onehot(iota((BE, NL * CAP), 1) + E == col), cot_recv[...].reshape(NL * CAP, D))
        grad_ac = (mirror * INV_ROOT * slope(dot(st, w_up[1]))).astype(BF)
        up[:TW, :] += dot_tn(st, grad_ca)
        up[TW:, :] += dot_tn(st, grad_ac)
        own = dot_nt(grad_ca, jnp.concatenate([w_up[0]] * 4, axis=0))
        back = dot_nt(grad_ac, jnp.concatenate([w_up[1]] * 4, axis=0)).astype(BF)
        grad_state = (own + back.astype(F32)).astype(BF)
        spread = onehot(iota((4 * BE, BE), 0) // 4 == iota((4 * BE, BE), 1))
        big = dot(spread, grad_state)
        big = jnp.where(lax.rem(iota((4 * BE, 256), 0), 4) == iota((4 * BE, 256), 1) // 64, big, 0.0)
        big = big.astype(BF)
        gsx[pl.ds(tall, 4 * BE), :] = big
        bil[...] += dot_tn(big, outer[pl.ds(tall, 4 * BE), :])

    @pl.when(step == BACK - 1)
    def _():
        turned = (up[...] * factor).T.astype(BF)
        for i in range(32):
            early[i, :, 1024:1152] = turned[16 * i : 16 * i + 16]
            r, c = (i % 2) * 128, (i // 2) * 128
            for j in range(8):
                early[i, :, 128 * j : 128 * j + 128] = (
                    bil[r + 16 * j : r + 16 * j + 16, c : c + 128] * factor
                ).astype(BF)

        def begin(d, carry):
            early_copy(d).start()
            return carry

        lax.fori_loop(1, n, begin, 0)

    @pl.when(step == SWAP)
    def _():
        def take(d, total_):
            early_copy(d).wait()
            return total_ + in_e[d].astype(F32)

        dp_e[0] = lax.fori_loop(1, n, take, early[me].astype(F32)).astype(BF)
        for c in swap(0, dp_e):
            c.start()

    @pl.when(step >= BACK)
    def _():
        part = step - BACK
        go[...] = dot_nt(gsx[pl.ds(pl.multiple_of(part * (32 * GS), 32 * GS), 32 * GS), :], wp[...]).astype(BF)

    @pl.when(step >= BACK)
    def _():
        part = step - BACK
        e_lane = lax.rem(iota((8, T), 1), 4)
        upper = e_lane >= 2
        odd = lax.rem(e_lane, 2) == 1
        stay = (iota((8, T), 0) >= 4) == odd

        def some(j, carry):
            hots, sides = [], []
            for i in range(BP):
                g = j * BP + i
                row = idx[pl.ds(part * GS + g, 1), :]
                hots.append(onehot(iota((256, T), 0) == jnp.bitwise_and(row, 255)))
                hi_of = jnp.right_shift(row, 8)
                lhs = jnp.concatenate(
                    [
                        jnp.concatenate(
                            [
                                go[pl.ds(pl.multiple_of(g * 32 + 16 * q, 16), 16), 128 * ch : 128 * ch + 128]
                                for q in range(2)
                            ],
                            axis=1,
                        )
                        for ch in range(16)
                    ],
                    axis=0,
                )
                at = pl.multiple_of((part * GS + g) * T, T)
                zero = jnp.zeros((128, 128), BF)
                side = jnp.concatenate(
                    [
                        jnp.concatenate([bas[pl.ds(at, 128), :], zero], axis=1),
                        jnp.concatenate([zero, bas[pl.ds(at + 128, 128), :]], axis=1),
                    ],
                    axis=0,
                )
                full = dot_nt(lhs, side)
                picked = [
                    jnp.where(upper, full[16 * ch + 8 : 16 * ch + 16], full[16 * ch : 16 * ch + 8])
                    for ch in range(16)
                ]
                grads = []
                for v in range(8):
                    z0, z1 = picked[2 * v], picked[2 * v + 1]
                    here = jnp.where(odd, z1, z0)
                    there = jnp.where(odd, z0, z1)
                    grads.append(jnp.where(stay, here, pltpu.roll(there, 4, 0)))
                grad = jnp.concatenate(grads, axis=0).astype(BF)
                sides.append(
                    jnp.concatenate([grad * onehot(hi_of == hi) for hi in range(8)], axis=0)
                )
            acc[...] += dot_nt(jnp.concatenate(sides, axis=1), jnp.concatenate(hots, axis=1))
            return carry

        lax.fori_loop(0, GS // BP, some, 0)

    @pl.when(step == ALL - 1)
    def _():
        def back(o):
            return remote(ret_send.at[o], ret_recv.at[o], r_send.at[o], r_recv.at[o], graph_at(-shifts[o]))

        for o in range(NL):
            part = acc[64 * (4 + o) : 64 * (4 + o) + 64, :]
            ret_send[o] = jnp.concatenate([part[:, :128], part[:, 128:]], axis=0).T.astype(BF)
            back(o).start()
        for i in range(4):
            m = pl.ds(256 * i, 256)
            pre_edge = dot(msg[m, :], w_edge[...])
            s_edge[m, :] = slope(pre_edge)
            hidden = silu(pre_edge).astype(BF)
            hid[m, :] = hidden
            s_down[m, :] = slope(dot_nt(hidden, w_down[...]))
        hots, backs = [], []
        for o in range(NL):
            picks = jnp.where(iota((1, CAP), 1) < count[0, o], rows[o : o + 1, :], -1)
            hots.append(onehot(iota((E, CAP), 0) == picks))
        for o in range(NL):
            back(o).wait()
            backs.append(unfold(ret_recv[o]))
        far = dot(jnp.concatenate(hots, axis=1), jnp.concatenate(backs, axis=0))
        downs = jnp.zeros((D, TW), F32)
        for i in range(4):
            m = pl.ds(256 * i, 256)
            part = acc[64 * i : 64 * i + 64, :]
            own = jnp.concatenate([part[:, :128], part[:, 128:]], axis=0).T
            grad_down = ((far[256 * i : 256 * i + 256] + unfold(own)) * s_down[m, :]).astype(BF)
            downs = downs + dot_tn(hid[m, :], grad_down)
            gedge[m, :] = (dot(grad_down, w_down[...]) * s_edge[m, :]).astype(BF)
        sibling = (dp, me + 1 - 2 * core)
        quarter = chips // 4

        def pair(j):
            part = pl.ds(quarter * j, quarter)
            return remote(late.at[1 - core, part], pair_in.at[part], p_send.at[j], p_recv.at[j], sibling)

        def pass_on(j):
            pair(j).wait()
            part = pl.ds(quarter * j, quarter)
            pair_out[part] = (late[core, part].astype(F32) + pair_in[part].astype(F32)).astype(BF)
            for i in range(quarter):
                to = quarter * j + i

                @pl.when(to != chip)
                def _():
                    d = lax.rem(to - chip + chips, chips)
                    late_copy(to, d).start()

        for j in range(4):
            edges = dot_tn(msg[:, 128 * j : 128 * j + 128], gedge[...])
            both = jnp.concatenate(
                [
                    edges * factor,
                    downs[128 * j : 128 * j + 128] * factor,
                    jnp.zeros((128, TW), F32),
                ],
                axis=1,
            ).astype(BF)
            for i in range(8):
                late[i % 2, quarter * j + i // 2] = both[16 * i : 16 * i + 16]
            pair(j).start()
            if j > 0:
                pass_on(j - 1)
        pass_on(3)
        for i in range(4):
            m = pl.ds(256 * i, 256)
            grad_msg[m, :] = dot_nt(gedge[m, :], w_edge[...]).astype(BF)
        for c in swap(0, dp_e):
            c.wait()
        sum_e[...] = total(dp_e)

        def take(d, total_):
            late_copy(lax.rem(chip + d, chips), d).wait()
            return total_ + in_l[d].astype(F32)

        dp_l[0] = lax.fori_loop(1, chips, take, pair_out[chip].astype(F32)).astype(BF)
        for c in swap(1, dp_l):
            c.start()
        for c in swap(1, dp_l):
            c.wait()
        sum_l[...] = total(dp_l)


def run(factor, msg, cot, w_edge, w_down, w_up, rows, rev, count, live, basis, idx, w_bil):
    whole = lambda shape: pl.BlockSpec(
        shape, lambda i: (0,) * len(shape), pipeline_mode=pl.Buffered(1)
    )
    smem = pl.BlockSpec(memory_space=pltpu.SMEM)
    n = lax.axis_size("graph")
    n_dp = lax.axis_size("dp")
    dma = pltpu.SemaphoreType.DMA
    bf = lambda *shape: pltpu.VMEM(shape, BF)
    f32 = lambda *shape: pltpu.VMEM(shape, F32)
    return pl.pallas_call(
        functools.partial(kernel, factor, n, n_dp),
        grid=(ALL,),
        out_shape=[
            jax.ShapeDtypeStruct((E, D), BF),
            jax.ShapeDtypeStruct((16, 1152), F32),
            jax.ShapeDtypeStruct((16, 640), F32),
        ],
        in_specs=[
            whole((E, D)), whole((E, D)), whole((D, D)), whole((TW, D)), whole((2, TW, D)),
            whole((NL, CAP)), whole((8, 128)), smem, smem,
            pl.BlockSpec((G * GS, K * B), lambda i: (jnp.minimum(i, STEPS - 1), 0)),
            whole((E // G, T)), whole((B, 4096)),
        ],
        out_specs=[whole((E, D)), whole((16, 1152)), whole((16, 640))],
        scratch_shapes=[
            bf(E, TW), bf(512, 256), bf(2048, 256), f32(32 * GS, 128),
            bf(4 * E, 2048), bf(E * K, 128), bf(E, 128),
            bf(NL, 128, 128), bf(NL, 128, 128), bf(NL, CAP, D), bf(NL, CAP, D),
            bf(4 * E, 256), f32(256, 2048), f32(2 * TW, D), bf(n, 16, 1152),
            bf(32 * GS, 2048), f32(512, 256), bf(NL, 128, 128), bf(NL, 128, 128),
            f32(E, D), bf(E, D), f32(E, TW), bf(E, D),
            bf(2, n // 2, 16, 640), bf(n, 16, 1152),
            bf(n // 2, 16, 640), bf(n // 2, 16, 640), bf(n // 2, 16, 640),
            bf(n_dp, 16, 1152), bf(n_dp, 16, 640),
            dma((2, NL)), dma((2, NL)), dma((n,)), dma((n,)), dma((n // 2,)), dma((n // 2,)),
            dma((NL,)), dma((NL,)), dma((4,)), dma((4,)), dma((2, n_dp)), dma((2, n_dp)),
        ],
        compiler_params=pltpu.CompilerParams(
            collective_id=0, has_side_effects=True, vmem_limit_bytes=VMEM_LIMIT
        ),
        name="triplets",
    )(msg, cot, w_edge, w_down, w_up, rows, rev, count, live, basis, idx, w_bil)


def last_kernel(grad_msg, e, l, o_msg, o_edge, o_down, o_bil, o_up):
    o_msg[...] = grad_msg[...]

    @pl.when(pl.program_id(0) == 0)
    def _():
        o_edge[...] = l[:, :D]
        o_down[...] = l[:, D : D + TW]
        square = jnp.concatenate([e[:, 128 * j : 128 * j + 128] for j in range(8)], axis=0).T
        o_bil[...] = square[:B]
        o_up[0] = e[:, 1024:1088]
        o_up[1] = e[:, 1088:1152]


def last(grad_msg, e, l):
    whole = lambda shape: pl.BlockSpec(shape, lambda i: (0,) * len(shape))
    rows = pl.BlockSpec((256, D), lambda i: (i, 0))
    return pl.pallas_call(
        last_kernel,
        grid=(4,),
        out_shape=[
            jax.ShapeDtypeStruct((E, D), BF),
            jax.ShapeDtypeStruct((16, D), F32),
            jax.ShapeDtypeStruct((16, TW), F32),
            jax.ShapeDtypeStruct((B, 128), F32),
            jax.ShapeDtypeStruct((2, 16, TW), F32),
        ],
        in_specs=[rows, whole((16, 1152)), whole((16, 640))],
        out_specs=[rows, whole((16, D)), whole((16, TW)), whole((B, 128)), whole((2, 16, TW))],
        name="outputs",
    )(grad_msg, e, l)


def body(
    messages, cotangent, triplet_basis, w_edge, w_down, w_bil, w_up,
    trip_src, send_rows, send_count, rev_src, edge_count,
):
    factor = 1.0 / math.sqrt(lax.axis_size("dp") * lax.axis_size("graph") * E)
    idx = trip_src[0].reshape(E // G, 2, 4, K).transpose(0, 1, 3, 2).reshape(E // G, T)
    grad_msg, e, l = run(
        factor, messages[0], cotangent[0], w_edge, w_down.T, w_up, send_rows[0],
        rev_src.reshape(8, 128), send_count, edge_count, triplet_basis[0], idx, w_bil,
    )
    grad_msg, g_edge, g_down, g_bil, g_up = last(grad_msg, e, l)
    return grad_msg[None], g_edge, g_down, g_bil, g_up.transpose(0, 2, 1)


def solution(mesh):
    row = P("dp", "graph", None)
    flat = P("dp", "graph")
    return jax.shard_map(
        body,
        mesh=mesh,
        in_specs=(row, row, row, P(), P(), P(), P(), row, row, flat, flat, flat),
        out_specs=(
            row,
            P("graph", None),
            P("graph", None),
            P(None, "graph"),
            P(None, None, "graph"),
        ),
        check_vma=False,
    )
```

```python
import functools
import math

import jax
import jax.numpy as jnp
from jax import lax
from jax.experimental import pallas as pl
from jax.experimental.pallas import tpu as pltpu
from jax.sharding import PartitionSpec as P

INV_ROOT = 0.7071067811865476
BF = jnp.bfloat16
F32 = jnp.float32
MESH = pl.DeviceIdType.MESH
VMEM_LIMIT = 56 * 1024 * 1024

E = 1024
K = 32
B = 112
TW = 64
D = 512
CAP = 256
NL = 4
G = 8
T = G * K


def offsets(count):
    return [(which // 2 + 1) * (1 - 2 * (which % 2)) for which in range(count)]


def sigmoid(v):
    return 0.5 + 0.5 * jnp.tanh(0.5 * v)


def silu(v):
    return v * sigmoid(v)


def slope(v):
    s = sigmoid(v)
    return s * (1.0 + v * (1.0 - s))


def iota(shape, dim):
    return lax.broadcasted_iota(jnp.int32, shape, dim)


def dot(a, b):
    return jnp.dot(a, b, preferred_element_type=F32)


def dot_nt(a, b):
    return lax.dot_general(a, b, (((1,), (1,)), ((), ())), preferred_element_type=F32)


def dot_tn(a, b):
    return lax.dot_general(a, b, (((0,), (0,)), ((), ())), preferred_element_type=F32)


def onehot(cond):
    return jnp.where(cond, 1.0, 0.0).astype(BF)


GS = 16
GP = 8
BP = 16
STEPS = E // (G * GS)


def graph_at(distance):
    n = lax.axis_size("graph")
    return (lax.axis_index("dp"), lax.rem(lax.axis_index("graph") + (distance + n), n))


def remote(src, dst, send, recv, where):
    return pltpu.make_async_remote_copy(
        src, dst, send, recv, device_id=where, device_id_type=MESH
    )


def greet(where):
    pl.semaphore_signal(
        pltpu.get_barrier_semaphore(), inc=1, device_id=where, device_id_type=MESH
    )


BE = 256
MIDDLE = STEPS
BACK = STEPS + E // BE
ALL = BACK + STEPS


def load_w(wp, w_bil):
    wp[...] = jnp.zeros_like(wp)
    for ch in range(16):
        wp[128 * ch : 128 * ch + B, :] = w_bil[:, 256 * ch : 256 * ch + 256]


def fold(rows):
    half = rows.shape[0] // 2
    return jnp.concatenate([rows[:half], rows[half:]], axis=1)


def unfold(rows):
    return jnp.concatenate([rows[:, :TW], rows[:, TW:]], axis=0)


def kernel(factor, n, n_dp, msg, cot, w_edge, w_down, w_up, rows, rev, count, live, basis, idx, w_bil,
           grad_msg, sum_e, sum_l,
           red, pool_t, wp, sbuf, outer, bas, state, red_send, red_recv, cot_send, cot_recv,
           gsx, bil, up, early, go, acc, ret_send, ret_recv, s_edge, hid, s_down, gedge,
           late, in_e, pair_in, pair_out, in_l, dp_e, dp_l,
           send, recv, e_send, e_recv, l_send, l_recv, r_send, r_recv, p_send, p_recv, d_send, d_recv):
    step = pl.program_id(0)
    shifts = offsets(NL)
    me = lax.axis_index("graph")
    dp = lax.axis_index("dp")
    core = lax.rem(me, 2)
    chip = me // 2
    chips = n // 2

    def red_copy(o):
        where = graph_at(shifts[o])
        return remote(red_send.at[o], red_recv.at[o], send.at[0, o], recv.at[0, o], where)

    def cot_copy(o):
        where = graph_at(shifts[o])
        return remote(cot_send.at[o], cot_recv.at[o], send.at[1, o], recv.at[1, o], where)

    def early_copy(d):
        to = lax.rem(me + d, n)
        return remote(early.at[to], in_e.at[d], e_send.at[d], e_recv.at[d], (dp, to))

    def late_copy(to, d):
        return remote(pair_out.at[to], in_l.at[d], l_send.at[d], l_recv.at[d], (dp, 2 * to + core))

    def swap(which, buf):
        out = []
        for d in range(1, n_dp):
            where = (lax.rem(dp + d, n_dp), me)
            out.append(remote(buf.at[0], buf.at[d], d_send.at[which, d], d_recv.at[which, d], where))
        return out

    def total(buf):
        terms = [buf[d].astype(F32) for d in range(n_dp)]
        out = jnp.zeros_like(terms[0])
        for source in range(n_dp):
            for d in range(n_dp):
                hit = lax.rem(dp + (n_dp - d), n_dp) == source
                out = out + jnp.where(hit, terms[d], 0.0)
        return out

    @pl.when(step == 0)
    def _():
        def hello(d, carry):
            greet((dp, lax.rem(me + d, n)))
            return carry

        lax.fori_loop(1, n, hello, 0)
        for d in range(1, n_dp):
            greet((lax.rem(dp + d, n_dp), me))
        for i in range(4):
            m = pl.ds(256 * i, 256)
            hidden = silu(dot(msg[m, :], w_edge[...])).astype(BF)
            red[m, :] = silu(dot_nt(hidden, w_down[...])).astype(BF)
        lane = iota((1, CAP), 1)
        lists = []
        for o in range(NL):
            lists.append(jnp.where(lane < count[0, o], rows[o : o + 1, :], -1))
        picks = jnp.concatenate(lists + lists, axis=0).T
        wide = iota((CAP, E), 1)
        for o in range(NL):
            red_send[o] = fold(dot(onehot(wide == picks[:, o : o + 1]), red[...]).astype(BF))
        pl.semaphore_wait(pltpu.get_barrier_semaphore(), n - 1 + n_dp - 1)
        for o in range(NL):
            red_copy(o).start()
        for o in range(NL):
            cot_send[o] = dot(onehot(wide == picks[:, o : o + 1]), cot[...]).astype(BF)
            cot_copy(o).start()
        load_w(wp, w_bil)
        for hi in range(8):
            if hi < 4:
                src = fold(red[256 * hi : 256 * hi + 256, :])
            else:
                red_copy(hi - 4).wait_recv()
                src = red_recv[hi - 4]
            flip = src.astype(F32).T
            pool_t[64 * hi : 64 * hi + 64, :] = jnp.concatenate(
                [flip[:64], flip[64:]], axis=1
            ).astype(BF)

        bil[...] = jnp.zeros_like(bil)
        up[...] = jnp.zeros_like(up)
        acc[...] = jnp.zeros_like(acc)

    @pl.when(step < MIDDLE)
    def _():
        part = step
        keep = onehot(lax.rem(iota((16, T), 1), 4) == iota((16, T), 0) // 4)
        low = iota((8, T), 0) < 4
        low1 = iota((8, 128), 0) < 4

        def some(j, carry):
            hots, his = [], []
            for i in range(GP):
                row = idx[pl.ds(part * GS + j * GP + i, 1), :]
                hots.append(onehot(iota((256, T), 0) == jnp.bitwise_and(row, 255)))
                his.append(jnp.right_shift(row, 8))
            found = dot(pool_t[...], jnp.concatenate(hots, axis=1)).astype(BF)
            founds = [found[:, T * i : T * i + T] for i in range(GP)]
            for i in range(GP):
                g = j * GP + i
                wide = basis[pl.ds(pl.multiple_of(g * G, G), G), :].astype(F32)
                pieces = []
                for k in range(K):
                    piece = wide[:, k * B : (k + 1) * B]
                    pieces.append(jnp.concatenate([piece, jnp.zeros((G, 128 - B), F32)], axis=1))
                first, second = [], []
                for k in range(0, K, 2):
                    x, y = pieces[k], pieces[k + 1]
                    z = pltpu.roll(jnp.where(low1, y, x), 4, 0)
                    first.append(jnp.where(low1, x, z))
                    second.append(jnp.where(low1, z, y))
                first = jnp.concatenate(first, axis=0).astype(BF)
                second = jnp.concatenate(second, axis=0).astype(BF)
                zero = jnp.zeros((128, 128), BF)
                at = pl.multiple_of((part * GS + g) * T, T)
                bas[pl.ds(at, 128), :] = first
                bas[pl.ds(at + 128, 128), :] = second
                rhs = jnp.concatenate(
                    [jnp.concatenate([first, zero], axis=1), jnp.concatenate([zero, second], axis=1)], axis=0
                )
                got = founds[i][:64] * onehot(his[i] == 0)
                for hi in range(1, 8):
                    got = got + founds[i][64 * hi : 64 * hi + 64] * onehot(his[i] == hi)
                got = got.astype(F32)
                tiles = []
                for v in range(8):
                    x = got[8 * v : 8 * v + 8]
                    y = pltpu.roll(x, 4, 0)
                    for d in (jnp.where(low, x, y), jnp.where(low, y, x)):
                        tiles.append(jnp.concatenate([d, d], axis=0).astype(BF) * keep)
                lhs = jnp.concatenate(tiles, axis=0)
                out = dot(lhs, rhs).astype(BF)
                for q in range(2):
                    for ch in range(16):
                        outer[pl.ds(pl.multiple_of((part * GS + g) * 32 + 16 * q, 16), 16), 128 * ch : 128 * ch + 128] = (
                            out[16 * ch : 16 * ch + 16, 128 * q : 128 * q + 128]
                        )
            return carry

        lax.fori_loop(0, GS // GP, some, 0)
        tall = 32 * GS
        full = dot(outer[pl.ds(pl.multiple_of(part * tall, tall), tall), :], wp[...])
        full = jnp.where(lax.rem(iota((tall, 256), 0), 4) == iota((tall, 256), 1) // 64, full, 0.0)
        full = full + pltpu.roll(full, 1, 0)
        full = full + pltpu.roll(full, 2, 0)
        sbuf[...] = full[:, :128] + full[:, 128:]
        picked = sbuf[pl.ds(3, G * GS, stride=4), :]
        state[pl.ds(pl.multiple_of(part * (G * GS), G * GS), G * GS), :] = (picked + pltpu.roll(picked, 64, 1)).astype(BF)

    @pl.when(step == MIDDLE)
    def _():
        for o in range(NL):
            red_copy(o).wait_send()
            cot_copy(o).wait()

    @pl.when((step >= MIDDLE) & (step < BACK))
    def _():
        part = step - MIDDLE
        at = pl.multiple_of(part * BE, BE)
        tall = pl.multiple_of(part * (4 * BE), 4 * BE)
        st = state[pl.ds(at, BE), :][:, :TW]
        alive = iota((BE, D), 0) + at < live[0, 0]
        scaled = jnp.where(alive, cot[pl.ds(at, BE), :].astype(F32) * INV_ROOT, 0.0)
        grad_ca = (scaled * slope(dot(st, w_up[0]))).astype(BF)
        col = jnp.concatenate(
            [
                jnp.concatenate([rev[pl.ds(part * (BE // 128) + h, 1), :]] * 8, axis=0).T[:, :1]
                for h in range(BE // 128)
            ],
            axis=0,
        )
        mirror = dot(onehot(iota((BE, E), 1) == col), cot[...])
        mirror = mirror + dot(onehot(iota((BE, NL * CAP), 1) + E == col), cot_recv[...].reshape(NL * CAP, D))
        grad_ac = (mirror * INV_ROOT * slope(dot(st, w_up[1]))).astype(BF)
        up[:TW, :] += dot_tn(st, grad_ca)
        up[TW:, :] += dot_tn(st, grad_ac)
        own = dot_nt(grad_ca, jnp.concatenate([w_up[0]] * 4, axis=0))
        back = dot_nt(grad_ac, jnp.concatenate([w_up[1]] * 4, axis=0)).astype(BF)
        grad_state = (own + back.astype(F32)).astype(BF)
        spread = onehot(iota((4 * BE, BE), 0) // 4 == iota((4 * BE, BE), 1))
        big = dot(spread, grad_state)
        big = jnp.where(lax.rem(iota((4 * BE, 256), 0), 4) == iota((4 * BE, 256), 1) // 64, big, 0.0)
        big = big.astype(BF)
        gsx[pl.ds(tall, 4 * BE), :] = big
        bil[...] += dot_tn(big, outer[pl.ds(tall, 4 * BE), :])

    @pl.when(step == BACK - 1)
    def _():
        turned = (up[...] * factor).T.astype(BF)
        for i in range(32):
            early[i, :, 1024:1152] = turned[16 * i : 16 * i + 16]
            r, c = (i % 2) * 128, (i // 2) * 128
            for j in range(8):
                early[i, :, 128 * j : 128 * j + 128] = (
                    bil[r + 16 * j : r + 16 * j + 16, c : c + 128] * factor
                ).astype(BF)

        def begin(d, carry):
            early_copy(d).start()
            return carry

        lax.fori_loop(1, n, begin, 0)

    @pl.when(step >= BACK)
    def _():
        part = step - BACK
        go[...] = dot_nt(gsx[pl.ds(pl.multiple_of(part * (32 * GS), 32 * GS), 32 * GS), :], wp[...]).astype(BF)

    @pl.when(step >= BACK)
    def _():
        part = step - BACK
        e_lane = lax.rem(iota((8, T), 1), 4)
        upper = e_lane >= 2
        odd = lax.rem(e_lane, 2) == 1
        stay = (iota((8, T), 0) >= 4) == odd

        def some(j, carry):
            hots, sides = [], []
            for i in range(BP):
                g = j * BP + i
                row = idx[pl.ds(part * GS + g, 1), :]
                hots.append(onehot(iota((256, T), 0) == jnp.bitwise_and(row, 255)))
                hi_of = jnp.right_shift(row, 8)
                lhs = jnp.concatenate(
                    [
                        jnp.concatenate(
                            [
                                go[pl.ds(pl.multiple_of(g * 32 + 16 * q, 16), 16), 128 * ch : 128 * ch + 128]
                                for q in range(2)
                            ],
                            axis=1,
                        )
                        for ch in range(16)
                    ],
                    axis=0,
                )
                at = pl.multiple_of((part * GS + g) * T, T)
                zero = jnp.zeros((128, 128), BF)
                side = jnp.concatenate(
                    [
                        jnp.concatenate([bas[pl.ds(at, 128), :], zero], axis=1),
                        jnp.concatenate([zero, bas[pl.ds(at + 128, 128), :]], axis=1),
                    ],
                    axis=0,
                )
                full = dot_nt(lhs, side)
                picked = [
                    jnp.where(upper, full[16 * ch + 8 : 16 * ch + 16], full[16 * ch : 16 * ch + 8])
                    for ch in range(16)
                ]
                grads = []
                for v in range(8):
                    z0, z1 = picked[2 * v], picked[2 * v + 1]
                    here = jnp.where(odd, z1, z0)
                    there = jnp.where(odd, z0, z1)
                    grads.append(jnp.where(stay, here, pltpu.roll(there, 4, 0)))
                grad = jnp.concatenate(grads, axis=0).astype(BF)
                sides.append(
                    jnp.concatenate([grad * onehot(hi_of == hi) for hi in range(8)], axis=0)
                )
            acc[...] += dot_nt(jnp.concatenate(sides, axis=1), jnp.concatenate(hots, axis=1))
            return carry

        lax.fori_loop(0, GS // BP, some, 0)

    @pl.when(step == ALL - 1)
    def _():
        def back(o):
            return remote(ret_send.at[o], ret_recv.at[o], r_send.at[o], r_recv.at[o], graph_at(-shifts[o]))

        for o in range(NL):
            part = acc[64 * (4 + o) : 64 * (4 + o) + 64, :]
            ret_send[o] = jnp.concatenate([part[:, :128], part[:, 128:]], axis=0).T.astype(BF)
            back(o).start()
        for i in range(4):
            m = pl.ds(256 * i, 256)
            pre_edge = dot(msg[m, :], w_edge[...])
            s_edge[m, :] = slope(pre_edge)
            hidden = silu(pre_edge).astype(BF)
            hid[m, :] = hidden
            s_down[m, :] = slope(dot_nt(hidden, w_down[...]))
        hots, backs = [], []
        for o in range(NL):
            picks = jnp.where(iota((1, CAP), 1) < count[0, o], rows[o : o + 1, :], -1)
            hots.append(onehot(iota((E, CAP), 0) == picks))
        for o in range(NL):
            back(o).wait()
            backs.append(unfold(ret_recv[o]))
        far = dot(jnp.concatenate(hots, axis=1), jnp.concatenate(backs, axis=0))
        downs = jnp.zeros((D, TW), F32)
        for i in range(4):
            m = pl.ds(256 * i, 256)
            part = acc[64 * i : 64 * i + 64, :]
            own = jnp.concatenate([part[:, :128], part[:, 128:]], axis=0).T
            grad_down = ((far[256 * i : 256 * i + 256] + unfold(own)) * s_down[m, :]).astype(BF)
            downs = downs + dot_tn(hid[m, :], grad_down)
            gedge[m, :] = (dot(grad_down, w_down[...]) * s_edge[m, :]).astype(BF)
        sibling = (dp, me + 1 - 2 * core)
        quarter = chips // 4

        def pair(j):
            part = pl.ds(quarter * j, quarter)
            return remote(late.at[1 - core, part], pair_in.at[part], p_send.at[j], p_recv.at[j], sibling)

        def pass_on(j):
            pair(j).wait()
            part = pl.ds(quarter * j, quarter)
            pair_out[part] = (late[core, part].astype(F32) + pair_in[part].astype(F32)).astype(BF)
            for i in range(quarter):
                to = quarter * j + i

                @pl.when(to != chip)
                def _():
                    d = lax.rem(to - chip + chips, chips)
                    late_copy(to, d).start()

        for j in range(4):
            edges = dot_tn(msg[:, 128 * j : 128 * j + 128], gedge[...])
            both = jnp.concatenate(
                [
                    edges * factor,
                    downs[128 * j : 128 * j + 128] * factor,
                    jnp.zeros((128, TW), F32),
                ],
                axis=1,
            ).astype(BF)
            for i in range(8):
                late[i % 2, quarter * j + i // 2] = both[16 * i : 16 * i + 16]
            pair(j).start()
            if j > 0:
                pass_on(j - 1)
        pass_on(3)
        for i in range(4):
            m = pl.ds(256 * i, 256)
            grad_msg[m, :] = dot_nt(gedge[m, :], w_edge[...]).astype(BF)

        def take_early(d, total_):
            early_copy(d).wait()
            return total_ + in_e[d].astype(F32)

        dp_e[0] = lax.fori_loop(1, n, take_early, early[me].astype(F32)).astype(BF)
        for c in swap(0, dp_e):
            c.start()

        def take(d, total_):
            late_copy(lax.rem(chip + d, chips), d).wait()
            return total_ + in_l[d].astype(F32)

        dp_l[0] = lax.fori_loop(1, chips, take, pair_out[chip].astype(F32)).astype(BF)
        for c in swap(1, dp_l):
            c.start()
        for c in swap(0, dp_e):
            c.wait()
        sum_e[...] = total(dp_e)
        for c in swap(1, dp_l):
            c.wait()
        sum_l[...] = total(dp_l)


def run(factor, msg, cot, w_edge, w_down, w_up, rows, rev, count, live, basis, idx, w_bil):
    whole = lambda shape: pl.BlockSpec(
        shape, lambda i: (0,) * len(shape), pipeline_mode=pl.Buffered(1)
    )
    smem = pl.BlockSpec(memory_space=pltpu.SMEM)
    n = lax.axis_size("graph")
    n_dp = lax.axis_size("dp")
    dma = pltpu.SemaphoreType.DMA
    bf = lambda *shape: pltpu.VMEM(shape, BF)
    f32 = lambda *shape: pltpu.VMEM(shape, F32)
    return pl.pallas_call(
        functools.partial(kernel, factor, n, n_dp),
        grid=(ALL,),
        out_shape=[
            jax.ShapeDtypeStruct((E, D), BF),
            jax.ShapeDtypeStruct((16, 1152), F32),
            jax.ShapeDtypeStruct((16, 640), F32),
        ],
        in_specs=[
            whole((E, D)), whole((E, D)), whole((D, D)), whole((TW, D)), whole((2, TW, D)),
            whole((NL, CAP)), whole((8, 128)), smem, smem,
            pl.BlockSpec((G * GS, K * B), lambda i: (jnp.minimum(i, STEPS - 1), 0)),
            whole((E // G, T)), whole((B, 4096)),
        ],
        out_specs=[whole((E, D)), whole((16, 1152)), whole((16, 640))],
        scratch_shapes=[
            bf(E, TW), bf(512, 256), bf(2048, 256), f32(32 * GS, 128),
            bf(4 * E, 2048), bf(E * K, 128), bf(E, 128),
            bf(NL, 128, 128), bf(NL, 128, 128), bf(NL, CAP, D), bf(NL, CAP, D),
            bf(4 * E, 256), f32(256, 2048), f32(2 * TW, D), bf(n, 16, 1152),
            bf(32 * GS, 2048), f32(512, 256), bf(NL, 128, 128), bf(NL, 128, 128),
            f32(E, D), bf(E, D), f32(E, TW), bf(E, D),
            bf(2, n // 2, 16, 640), bf(n, 16, 1152),
            bf(n // 2, 16, 640), bf(n // 2, 16, 640), bf(n // 2, 16, 640),
            bf(n_dp, 16, 1152), bf(n_dp, 16, 640),
            dma((2, NL)), dma((2, NL)), dma((n,)), dma((n,)), dma((n // 2,)), dma((n // 2,)),
            dma((NL,)), dma((NL,)), dma((4,)), dma((4,)), dma((2, n_dp)), dma((2, n_dp)),
        ],
        compiler_params=pltpu.CompilerParams(
            collective_id=0, has_side_effects=True, vmem_limit_bytes=VMEM_LIMIT
        ),
        name="triplets",
    )(msg, cot, w_edge, w_down, w_up, rows, rev, count, live, basis, idx, w_bil)


def last_kernel(grad_msg, e, l, o_msg, o_edge, o_down, o_bil, o_up):
    o_msg[...] = grad_msg[...]

    @pl.when(pl.program_id(0) == 0)
    def _():
        o_edge[...] = l[:, :D]
        o_down[...] = l[:, D : D + TW]
        square = jnp.concatenate([e[:, 128 * j : 128 * j + 128] for j in range(8)], axis=0).T
        o_bil[...] = square[:B]
        o_up[0] = e[:, 1024:1088]
        o_up[1] = e[:, 1088:1152]


def last(grad_msg, e, l):
    whole = lambda shape: pl.BlockSpec(shape, lambda i: (0,) * len(shape))
    rows = pl.BlockSpec((256, D), lambda i: (i, 0))
    return pl.pallas_call(
        last_kernel,
        grid=(4,),
        out_shape=[
            jax.ShapeDtypeStruct((E, D), BF),
            jax.ShapeDtypeStruct((16, D), F32),
            jax.ShapeDtypeStruct((16, TW), F32),
            jax.ShapeDtypeStruct((B, 128), F32),
            jax.ShapeDtypeStruct((2, 16, TW), F32),
        ],
        in_specs=[rows, whole((16, 1152)), whole((16, 640))],
        out_specs=[rows, whole((16, D)), whole((16, TW)), whole((B, 128)), whole((2, 16, TW))],
        name="outputs",
    )(grad_msg, e, l)


def body(
    messages, cotangent, triplet_basis, w_edge, w_down, w_bil, w_up,
    trip_src, send_rows, send_count, rev_src, edge_count,
):
    factor = 1.0 / math.sqrt(lax.axis_size("dp") * lax.axis_size("graph") * E)
    idx = trip_src[0].reshape(E // G, 2, 4, K).transpose(0, 1, 3, 2).reshape(E // G, T)
    grad_msg, e, l = run(
        factor, messages[0], cotangent[0], w_edge, w_down.T, w_up, send_rows[0],
        rev_src.reshape(8, 128), send_count, edge_count, triplet_basis[0], idx, w_bil,
    )
    grad_msg, g_edge, g_down, g_bil, g_up = last(grad_msg, e, l)
    return grad_msg[None], g_edge, g_down, g_bil, g_up.transpose(0, 2, 1)


def solution(mesh):
    row = P("dp", "graph", None)
    flat = P("dp", "graph")
    return jax.shard_map(
        body,
        mesh=mesh,
        in_specs=(row, row, row, P(), P(), P(), P(), row, row, flat, flat, flat),
        out_specs=(
            row,
            P("graph", None),
            P("graph", None),
            P(None, "graph"),
            P(None, None, "graph"),
        ),
        check_vma=False,
    )
```

```python
import functools
import math

import jax
import jax.numpy as jnp
from jax import lax
from jax.experimental import pallas as pl
from jax.experimental.pallas import tpu as pltpu
from jax.sharding import PartitionSpec as P

INV_ROOT = 0.7071067811865476
BF = jnp.bfloat16
F32 = jnp.float32
MESH = pl.DeviceIdType.MESH
VMEM_LIMIT = 56 * 1024 * 1024

E = 1024
K = 32
B = 112
TW = 64
D = 512
CAP = 256
NL = 4
G = 8
T = G * K


def offsets(count):
    return [(which // 2 + 1) * (1 - 2 * (which % 2)) for which in range(count)]


def sigmoid(v):
    return 0.5 + 0.5 * jnp.tanh(0.5 * v)


def silu(v):
    return v * sigmoid(v)


def slope(v):
    s = sigmoid(v)
    return s * (1.0 + v * (1.0 - s))


def iota(shape, dim):
    return lax.broadcasted_iota(jnp.int32, shape, dim)


def dot(a, b):
    return jnp.dot(a, b, preferred_element_type=F32)


def dot_nt(a, b):
    return lax.dot_general(a, b, (((1,), (1,)), ((), ())), preferred_element_type=F32)


def dot_tn(a, b):
    return lax.dot_general(a, b, (((0,), (0,)), ((), ())), preferred_element_type=F32)


def onehot(cond):
    return jnp.where(cond, 1.0, 0.0).astype(BF)


GS = 16
GP = 8
BP = 16
STEPS = E // (G * GS)


def graph_at(distance):
    n = lax.axis_size("graph")
    return (lax.axis_index("dp"), lax.rem(lax.axis_index("graph") + (distance + n), n))


def remote(src, dst, send, recv, where):
    return pltpu.make_async_remote_copy(
        src, dst, send, recv, device_id=where, device_id_type=MESH
    )


def greet(where):
    pl.semaphore_signal(
        pltpu.get_barrier_semaphore(), inc=1, device_id=where, device_id_type=MESH
    )


BE = 256
MIDDLE = STEPS
BACK = STEPS + E // BE
ALL = BACK + STEPS


def load_w(wp, w_bil):
    wp[...] = jnp.zeros_like(wp)
    for ch in range(16):
        wp[128 * ch : 128 * ch + B, :] = w_bil[:, 256 * ch : 256 * ch + 256]


def fold(rows):
    half = rows.shape[0] // 2
    return jnp.concatenate([rows[:half], rows[half:]], axis=1)


def unfold(rows):
    return jnp.concatenate([rows[:, :TW], rows[:, TW:]], axis=0)


def kernel(factor, n, n_dp, msg, cot, w_edge, w_down, w_up, rows, rev, count, live, basis, idx, w_bil,
           gedge, sum_e, sum_l,
           red, pool_t, wp, sbuf, outer, bas, state, red_send, red_recv, cot_send, cot_recv,
           gsx, bil, up, early, go, acc, ret_send, ret_recv, s_edge, hid, s_down,
           late, in_e, pair_in, pair_out, in_l, dp_e, dp_l,
           send, recv, e_send, e_recv, l_send, l_recv, r_send, r_recv, p_send, p_recv, d_send, d_recv):
    step = pl.program_id(0)
    shifts = offsets(NL)
    me = lax.axis_index("graph")
    dp = lax.axis_index("dp")
    core = lax.rem(me, 2)
    chip = me // 2
    chips = n // 2

    def red_copy(o):
        where = graph_at(shifts[o])
        return remote(red_send.at[o], red_recv.at[o], send.at[0, o], recv.at[0, o], where)

    def cot_copy(o):
        where = graph_at(shifts[o])
        return remote(cot_send.at[o], cot_recv.at[o], send.at[1, o], recv.at[1, o], where)

    def early_copy(d):
        to = lax.rem(me + d, n)
        return remote(early.at[to], in_e.at[d], e_send.at[d], e_recv.at[d], (dp, to))

    def late_copy(to, d):
        return remote(pair_out.at[to], in_l.at[d], l_send.at[d], l_recv.at[d], (dp, 2 * to + core))

    def swap(which, buf):
        out = []
        for d in range(1, n_dp):
            where = (lax.rem(dp + d, n_dp), me)
            out.append(remote(buf.at[0], buf.at[d], d_send.at[which, d], d_recv.at[which, d], where))
        return out

    def total(buf):
        terms = [buf[d].astype(F32) for d in range(n_dp)]
        out = jnp.zeros_like(terms[0])
        for source in range(n_dp):
            for d in range(n_dp):
                hit = lax.rem(dp + (n_dp - d), n_dp) == source
                out = out + jnp.where(hit, terms[d], 0.0)
        return out

    @pl.when(step == 0)
    def _():
        def hello(d, carry):
            greet((dp, lax.rem(me + d, n)))
            return carry

        lax.fori_loop(1, n, hello, 0)
        for d in range(1, n_dp):
            greet((lax.rem(dp + d, n_dp), me))
        for i in range(4):
            m = pl.ds(256 * i, 256)
            hidden = silu(dot(msg[m, :], w_edge[...])).astype(BF)
            red[m, :] = silu(dot_nt(hidden, w_down[...])).astype(BF)
        lane = iota((1, CAP), 1)
        lists = []
        for o in range(NL):
            lists.append(jnp.where(lane < count[0, o], rows[o : o + 1, :], -1))
        picks = jnp.concatenate(lists + lists, axis=0).T
        wide = iota((CAP, E), 1)
        for o in range(NL):
            red_send[o] = fold(dot(onehot(wide == picks[:, o : o + 1]), red[...]).astype(BF))
        pl.semaphore_wait(pltpu.get_barrier_semaphore(), n - 1 + n_dp - 1)
        for o in range(NL):
            red_copy(o).start()
        for o in range(NL):
            cot_send[o] = dot(onehot(wide == picks[:, o : o + 1]), cot[...]).astype(BF)
            cot_copy(o).start()
        load_w(wp, w_bil)
        for hi in range(8):
            if hi < 4:
                src = fold(red[256 * hi : 256 * hi + 256, :])
            else:
                red_copy(hi - 4).wait_recv()
                src = red_recv[hi - 4]
            flip = src.astype(F32).T
            pool_t[64 * hi : 64 * hi + 64, :] = jnp.concatenate(
                [flip[:64], flip[64:]], axis=1
            ).astype(BF)

        bil[...] = jnp.zeros_like(bil)
        up[...] = jnp.zeros_like(up)
        acc[...] = jnp.zeros_like(acc)

    @pl.when(step < MIDDLE)
    def _():
        part = step
        keep = onehot(lax.rem(iota((16, T), 1), 4) == iota((16, T), 0) // 4)
        low = iota((8, T), 0) < 4
        low1 = iota((8, 128), 0) < 4

        def some(j, carry):
            hots, his = [], []
            for i in range(GP):
                row = idx[pl.ds(part * GS + j * GP + i, 1), :]
                hots.append(onehot(iota((256, T), 0) == jnp.bitwise_and(row, 255)))
                his.append(jnp.right_shift(row, 8))
            found = dot(pool_t[...], jnp.concatenate(hots, axis=1)).astype(BF)
            founds = [found[:, T * i : T * i + T] for i in range(GP)]
            for i in range(GP):
                g = j * GP + i
                wide = basis[pl.ds(pl.multiple_of(g * G, G), G), :].astype(F32)
                pieces = []
                for k in range(K):
                    piece = wide[:, k * B : (k + 1) * B]
                    pieces.append(jnp.concatenate([piece, jnp.zeros((G, 128 - B), F32)], axis=1))
                first, second = [], []
                for k in range(0, K, 2):
                    x, y = pieces[k], pieces[k + 1]
                    z = pltpu.roll(jnp.where(low1, y, x), 4, 0)
                    first.append(jnp.where(low1, x, z))
                    second.append(jnp.where(low1, z, y))
                first = jnp.concatenate(first, axis=0).astype(BF)
                second = jnp.concatenate(second, axis=0).astype(BF)
                zero = jnp.zeros((128, 128), BF)
                at = pl.multiple_of((part * GS + g) * T, T)
                bas[pl.ds(at, 128), :] = first
                bas[pl.ds(at + 128, 128), :] = second
                rhs = jnp.concatenate(
                    [jnp.concatenate([first, zero], axis=1), jnp.concatenate([zero, second], axis=1)], axis=0
                )
                got = founds[i][:64] * onehot(his[i] == 0)
                for hi in range(1, 8):
                    got = got + founds[i][64 * hi : 64 * hi + 64] * onehot(his[i] == hi)
                got = got.astype(F32)
                tiles = []
                for v in range(8):
                    x = got[8 * v : 8 * v + 8]
                    y = pltpu.roll(x, 4, 0)
                    for d in (jnp.where(low, x, y), jnp.where(low, y, x)):
                        tiles.append(jnp.concatenate([d, d], axis=0).astype(BF) * keep)
                lhs = jnp.concatenate(tiles, axis=0)
                out = dot(lhs, rhs).astype(BF)
                for q in range(2):
                    for ch in range(16):
                        outer[pl.ds(pl.multiple_of((part * GS + g) * 32 + 16 * q, 16), 16), 128 * ch : 128 * ch + 128] = (
                            out[16 * ch : 16 * ch + 16, 128 * q : 128 * q + 128]
                        )
            return carry

        lax.fori_loop(0, GS // GP, some, 0)
        tall = 32 * GS
        full = dot(outer[pl.ds(pl.multiple_of(part * tall, tall), tall), :], wp[...])
        full = jnp.where(lax.rem(iota((tall, 256), 0), 4) == iota((tall, 256), 1) // 64, full, 0.0)
        full = full + pltpu.roll(full, 1, 0)
        full = full + pltpu.roll(full, 2, 0)
        sbuf[...] = full[:, :128] + full[:, 128:]
        picked = sbuf[pl.ds(3, G * GS, stride=4), :]
        state[pl.ds(pl.multiple_of(part * (G * GS), G * GS), G * GS), :] = (picked + pltpu.roll(picked, 64, 1)).astype(BF)

    @pl.when(step == MIDDLE)
    def _():
        for o in range(NL):
            red_copy(o).wait_send()
            cot_copy(o).wait()

    @pl.when((step >= MIDDLE) & (step < BACK))
    def _():
        part = step - MIDDLE
        at = pl.multiple_of(part * BE, BE)
        tall = pl.multiple_of(part * (4 * BE), 4 * BE)
        st = state[pl.ds(at, BE), :][:, :TW]
        alive = iota((BE, D), 0) + at < live[0, 0]
        scaled = jnp.where(alive, cot[pl.ds(at, BE), :].astype(F32) * INV_ROOT, 0.0)
        grad_ca = (scaled * slope(dot(st, w_up[0]))).astype(BF)
        col = jnp.concatenate(
            [
                jnp.concatenate([rev[pl.ds(part * (BE // 128) + h, 1), :]] * 8, axis=0).T[:, :1]
                for h in range(BE // 128)
            ],
            axis=0,
        )
        mirror = dot(onehot(iota((BE, E), 1) == col), cot[...])
        mirror = mirror + dot(onehot(iota((BE, NL * CAP), 1) + E == col), cot_recv[...].reshape(NL * CAP, D))
        grad_ac = (mirror * INV_ROOT * slope(dot(st, w_up[1]))).astype(BF)
        up[:TW, :] += dot_tn(st, grad_ca)
        up[TW:, :] += dot_tn(st, grad_ac)
        own = dot_nt(grad_ca, jnp.concatenate([w_up[0]] * 4, axis=0))
        back = dot_nt(grad_ac, jnp.concatenate([w_up[1]] * 4, axis=0)).astype(BF)
        grad_state = (own + back.astype(F32)).astype(BF)
        spread = onehot(iota((4 * BE, BE), 0) // 4 == iota((4 * BE, BE), 1))
        big = dot(spread, grad_state)
        big = jnp.where(lax.rem(iota((4 * BE, 256), 0), 4) == iota((4 * BE, 256), 1) // 64, big, 0.0)
        big = big.astype(BF)
        gsx[pl.ds(tall, 4 * BE), :] = big
        bil[...] += dot_tn(big, outer[pl.ds(tall, 4 * BE), :])

    @pl.when(step == BACK - 1)
    def _():
        turned = (up[...] * factor).T.astype(BF)
        for i in range(32):
            early[i, :, 1024:1152] = turned[16 * i : 16 * i + 16]
            r, c = (i % 2) * 128, (i // 2) * 128
            for j in range(8):
                early[i, :, 128 * j : 128 * j + 128] = (
                    bil[r + 16 * j : r + 16 * j + 16, c : c + 128] * factor
                ).astype(BF)

        def begin(d, carry):
            early_copy(d).start()
            return carry

        lax.fori_loop(1, n, begin, 0)

    @pl.when(step >= BACK)
    def _():
        part = step - BACK
        go[...] = dot_nt(gsx[pl.ds(pl.multiple_of(part * (32 * GS), 32 * GS), 32 * GS), :], wp[...]).astype(BF)

    @pl.when(step >= BACK)
    def _():
        part = step - BACK
        e_lane = lax.rem(iota((8, T), 1), 4)
        upper = e_lane >= 2
        odd = lax.rem(e_lane, 2) == 1
        stay = (iota((8, T), 0) >= 4) == odd

        def some(j, carry):
            hots, sides = [], []
            for i in range(BP):
                g = j * BP + i
                row = idx[pl.ds(part * GS + g, 1), :]
                hots.append(onehot(iota((256, T), 0) == jnp.bitwise_and(row, 255)))
                hi_of = jnp.right_shift(row, 8)
                lhs = jnp.concatenate(
                    [
                        jnp.concatenate(
                            [
                                go[pl.ds(pl.multiple_of(g * 32 + 16 * q, 16), 16), 128 * ch : 128 * ch + 128]
                                for q in range(2)
                            ],
                            axis=1,
                        )
                        for ch in range(16)
                    ],
                    axis=0,
                )
                at = pl.multiple_of((part * GS + g) * T, T)
                zero = jnp.zeros((128, 128), BF)
                side = jnp.concatenate(
                    [
                        jnp.concatenate([bas[pl.ds(at, 128), :], zero], axis=1),
                        jnp.concatenate([zero, bas[pl.ds(at + 128, 128), :]], axis=1),
                    ],
                    axis=0,
                )
                full = dot_nt(lhs, side)
                picked = [
                    jnp.where(upper, full[16 * ch + 8 : 16 * ch + 16], full[16 * ch : 16 * ch + 8])
                    for ch in range(16)
                ]
                grads = []
                for v in range(8):
                    z0, z1 = picked[2 * v], picked[2 * v + 1]
                    here = jnp.where(odd, z1, z0)
                    there = jnp.where(odd, z0, z1)
                    grads.append(jnp.where(stay, here, pltpu.roll(there, 4, 0)))
                grad = jnp.concatenate(grads, axis=0).astype(BF)
                sides.append(
                    jnp.concatenate([grad * onehot(hi_of == hi) for hi in range(8)], axis=0)
                )
            acc[...] += dot_nt(jnp.concatenate(sides, axis=1), jnp.concatenate(hots, axis=1))
            return carry

        lax.fori_loop(0, GS // BP, some, 0)

    @pl.when(step == ALL - 1)
    def _():
        def back(o):
            return remote(ret_send.at[o], ret_recv.at[o], r_send.at[o], r_recv.at[o], graph_at(-shifts[o]))

        for o in range(NL):
            part = acc[64 * (4 + o) : 64 * (4 + o) + 64, :]
            ret_send[o] = jnp.concatenate([part[:, :128], part[:, 128:]], axis=0).T.astype(BF)
            back(o).start()
        for i in range(4):
            m = pl.ds(256 * i, 256)
            pre_edge = dot(msg[m, :], w_edge[...])
            s_edge[m, :] = slope(pre_edge)
            hidden = silu(pre_edge).astype(BF)
            hid[m, :] = hidden
            s_down[m, :] = slope(dot_nt(hidden, w_down[...]))
        hots, backs = [], []
        for o in range(NL):
            picks = jnp.where(iota((1, CAP), 1) < count[0, o], rows[o : o + 1, :], -1)
            hots.append(onehot(iota((E, CAP), 0) == picks))
        for o in range(NL):
            back(o).wait()
            backs.append(unfold(ret_recv[o]))
        far = dot(jnp.concatenate(hots, axis=1), jnp.concatenate(backs, axis=0))
        downs = jnp.zeros((D, TW), F32)
        for i in range(4):
            m = pl.ds(256 * i, 256)
            part = acc[64 * i : 64 * i + 64, :]
            own = jnp.concatenate([part[:, :128], part[:, 128:]], axis=0).T
            grad_down = ((far[256 * i : 256 * i + 256] + unfold(own)) * s_down[m, :]).astype(BF)
            downs = downs + dot_tn(hid[m, :], grad_down)
            gedge[m, :] = (dot(grad_down, w_down[...]) * s_edge[m, :]).astype(BF)
        sibling = (dp, me + 1 - 2 * core)
        quarter = chips // 4

        def pair(j):
            part = pl.ds(quarter * j, quarter)
            return remote(late.at[1 - core, part], pair_in.at[part], p_send.at[j], p_recv.at[j], sibling)

        def pass_on(j):
            pair(j).wait()
            part = pl.ds(quarter * j, quarter)
            pair_out[part] = (late[core, part].astype(F32) + pair_in[part].astype(F32)).astype(BF)
            for i in range(quarter):
                to = quarter * j + i

                @pl.when(to != chip)
                def _():
                    d = lax.rem(to - chip + chips, chips)
                    late_copy(to, d).start()

        for j in range(4):
            edges = dot_tn(msg[:, 128 * j : 128 * j + 128], gedge[...])
            both = jnp.concatenate(
                [
                    edges * factor,
                    downs[128 * j : 128 * j + 128] * factor,
                    jnp.zeros((128, TW), F32),
                ],
                axis=1,
            ).astype(BF)
            for i in range(8):
                late[i % 2, quarter * j + i // 2] = both[16 * i : 16 * i + 16]
            pair(j).start()
            if j > 0:
                pass_on(j - 1)
        pass_on(3)

        def take_early(d, total_):
            early_copy(d).wait()
            return total_ + in_e[d].astype(F32)

        dp_e[0] = lax.fori_loop(1, n, take_early, early[me].astype(F32)).astype(BF)
        for c in swap(0, dp_e):
            c.start()

        def take(d, total_):
            late_copy(lax.rem(chip + d, chips), d).wait()
            return total_ + in_l[d].astype(F32)

        dp_l[0] = lax.fori_loop(1, chips, take, pair_out[chip].astype(F32)).astype(BF)
        for c in swap(1, dp_l):
            c.start()
        for c in swap(0, dp_e):
            c.wait()
        sum_e[...] = total(dp_e)
        for c in swap(1, dp_l):
            c.wait()
        sum_l[...] = total(dp_l)


def run(factor, msg, cot, w_edge, w_down, w_up, rows, rev, count, live, basis, idx, w_bil):
    whole = lambda shape: pl.BlockSpec(
        shape, lambda i: (0,) * len(shape), pipeline_mode=pl.Buffered(1)
    )
    smem = pl.BlockSpec(memory_space=pltpu.SMEM)
    n = lax.axis_size("graph")
    n_dp = lax.axis_size("dp")
    dma = pltpu.SemaphoreType.DMA
    bf = lambda *shape: pltpu.VMEM(shape, BF)
    f32 = lambda *shape: pltpu.VMEM(shape, F32)
    return pl.pallas_call(
        functools.partial(kernel, factor, n, n_dp),
        grid=(ALL,),
        out_shape=[
            jax.ShapeDtypeStruct((E, D), BF),
            jax.ShapeDtypeStruct((16, 1152), F32),
            jax.ShapeDtypeStruct((16, 640), F32),
        ],
        in_specs=[
            whole((E, D)), whole((E, D)), whole((D, D)), whole((TW, D)), whole((2, TW, D)),
            whole((NL, CAP)), whole((8, 128)), smem, smem,
            pl.BlockSpec((G * GS, K * B), lambda i: (jnp.minimum(i, STEPS - 1), 0)),
            whole((E // G, T)), whole((B, 4096)),
        ],
        out_specs=[whole((E, D)), whole((16, 1152)), whole((16, 640))],
        scratch_shapes=[
            bf(E, TW), bf(512, 256), bf(2048, 256), f32(32 * GS, 128),
            bf(4 * E, 2048), bf(E * K, 128), bf(E, 128),
            bf(NL, 128, 128), bf(NL, 128, 128), bf(NL, CAP, D), bf(NL, CAP, D),
            bf(4 * E, 256), f32(256, 2048), f32(2 * TW, D), bf(n, 16, 1152),
            bf(32 * GS, 2048), f32(512, 256), bf(NL, 128, 128), bf(NL, 128, 128),
            f32(E, D), bf(E, D), f32(E, TW),
            bf(2, n // 2, 16, 640), bf(n, 16, 1152),
            bf(n // 2, 16, 640), bf(n // 2, 16, 640), bf(n // 2, 16, 640),
            bf(n_dp, 16, 1152), bf(n_dp, 16, 640),
            dma((2, NL)), dma((2, NL)), dma((n,)), dma((n,)), dma((n // 2,)), dma((n // 2,)),
            dma((NL,)), dma((NL,)), dma((4,)), dma((4,)), dma((2, n_dp)), dma((2, n_dp)),
        ],
        compiler_params=pltpu.CompilerParams(
            collective_id=0, has_side_effects=True, vmem_limit_bytes=VMEM_LIMIT
        ),
        name="triplets",
    )(msg, cot, w_edge, w_down, w_up, rows, rev, count, live, basis, idx, w_bil)


def last_kernel(gedge, w_edge, e, l, o_msg, o_edge, o_down, o_bil, o_up):
    o_msg[...] = dot_nt(gedge[...], w_edge[...]).astype(BF)

    @pl.when(pl.program_id(0) == 0)
    def _():
        o_edge[...] = l[:, :D]
        o_down[...] = l[:, D : D + TW]
        square = jnp.concatenate([e[:, 128 * j : 128 * j + 128] for j in range(8)], axis=0).T
        o_bil[...] = square[:B]
        o_up[0] = e[:, 1024:1088]
        o_up[1] = e[:, 1088:1152]


def last(gedge, w_edge, e, l):
    whole = lambda shape: pl.BlockSpec(shape, lambda i: (0,) * len(shape))
    rows = pl.BlockSpec((512, D), lambda i: (i, 0))
    return pl.pallas_call(
        last_kernel,
        grid=(2,),
        out_shape=[
            jax.ShapeDtypeStruct((E, D), BF),
            jax.ShapeDtypeStruct((16, D), F32),
            jax.ShapeDtypeStruct((16, TW), F32),
            jax.ShapeDtypeStruct((B, 128), F32),
            jax.ShapeDtypeStruct((2, 16, TW), F32),
        ],
        in_specs=[rows, whole((D, D)), whole((16, 1152)), whole((16, 640))],
        out_specs=[rows, whole((16, D)), whole((16, TW)), whole((B, 128)), whole((2, 16, TW))],
        name="outputs",
    )(gedge, w_edge, e, l)


def body(
    messages, cotangent, triplet_basis, w_edge, w_down, w_bil, w_up,
    trip_src, send_rows, send_count, rev_src, edge_count,
):
    factor = 1.0 / math.sqrt(lax.axis_size("dp") * lax.axis_size("graph") * E)
    idx = trip_src[0].reshape(E // G, 2, 4, K).transpose(0, 1, 3, 2).reshape(E // G, T)
    gedge, e, l = run(
        factor, messages[0], cotangent[0], w_edge, w_down.T, w_up, send_rows[0],
        rev_src.reshape(8, 128), send_count, edge_count, triplet_basis[0], idx, w_bil,
    )
    grad_msg, g_edge, g_down, g_bil, g_up = last(gedge, w_edge, e, l)
    return grad_msg[None], g_edge, g_down, g_bil, g_up.transpose(0, 2, 1)


def solution(mesh):
    row = P("dp", "graph", None)
    flat = P("dp", "graph")
    return jax.shard_map(
        body,
        mesh=mesh,
        in_specs=(row, row, row, P(), P(), P(), P(), row, row, flat, flat, flat),
        out_specs=(
            row,
            P("graph", None),
            P("graph", None),
            P(None, "graph"),
            P(None, None, "graph"),
        ),
        check_vma=False,
    )
```
